256 devices in a mesh: feat: 8 (over y, core), node: 32 (over x, z).
Axes of the slice: x: 4, y: 4, z: 8, core: 2. Of those that a mesh axis runs over, the one named last changes fastest.
Arguments:
- node_feats: float32 [256, 131072], P('feat', 'node'), may hold values from -6 to 6
- tiles: float32 [1024, 4, 128, 128], P('node'), may hold values from -0.5 to 0.5
- send_col: int32 [1024, 4], P('node'), may hold values from 0 to 31
- recv_row: int32 [1024, 4], P('node'), may hold values from -1 to 31, as said below
- degree: int32 [131072], P('node'), may hold values from 1 to 8
- w_self: float32 [256, 256], replicated, may hold values from -0.375 to 0.375
- w_neigh: float32 [256, 256], replicated, may hold values from -0.375 to 0.375
- bias: float32 [256], replicated, may hold values from -3 to 3
- cotangent: float32 [131072, 256], P(('node', 'feat')), may hold values from -24 to 24
Outputs:
- activated: float32 [131072, 256], P(('node', 'feat'))
- grad_feats: float32 [256, 131072], P('feat', 'node')
- grad_self: float32 [256, 256], replicated
- grad_neigh: float32 [256, 256], replicated
- grad_bias: float32 [256], replicated
The draws below stay inside these ranges and needn't reach their ends.
Inputs may be any that keep to these rules, and one draw needn't show every extreme that they name: `recv_row`: at most 4 live slots from one sender to one owner; every sender fills all 4 slots to itself, and one owner receives 4 live slots from every sender; -1 marks an empty slot.
All inputs are finite; a program needn't handle non-finite values.
Results may differ from the reference program's by a relative error of at most 0.0003.
Values sent between devices are 32-bit elements; how exact they have to be, the bound alone decides.
A program may use at most 64 MiB of HBM per device.

```python
import jax
import jax.numpy as jnp
from jax import lax

H = 256
TB = 128
BLK_DEV = 32
CAP = 4
NODES = 131072
N_NODE = 32


def slot_rows(key):
    hot_owner = jax.random.randint(jax.random.fold_in(key, 11), (), 0, N_NODE)
    counts = jax.random.randint(jax.random.fold_in(key, 12), (N_NODE, N_NODE), 0, CAP + 1)
    senders = jnp.arange(N_NODE, dtype=jnp.int32)[:, None]
    owners = jnp.arange(N_NODE, dtype=jnp.int32)[None, :]
    filled = jnp.logical_or(owners == hot_owner, senders == owners)
    counts = jnp.where(filled, CAP, counts)
    live = jnp.arange(CAP, dtype=jnp.int32)[None, None, :] < counts[..., None]
    blocks = jax.random.randint(jax.random.fold_in(key, 13), (N_NODE, N_NODE, CAP), 0, BLK_DEV)
    return jnp.where(live, blocks, -1)


def draw_recv_row(key, part):
    layout = slot_rows(key)
    return layout.transpose(1, 0, 2).reshape(N_NODE * N_NODE, CAP).astype(jnp.int32)


def draw_send_col(key, part):
    key = jax.random.fold_in(key, 5)
    return jax.random.randint(key, (N_NODE * N_NODE, CAP), 0, BLK_DEV).astype(jnp.int32)


def place_ends(result, stream_key, low, high):
    place = [jax.random.randint(jax.random.fold_in(stream_key, axis), (), 0, length) for axis, length in enumerate(result.shape)]
    main_axis = result.shape.index(max(result.shape))
    beside = place[:main_axis] + [(place[main_axis] + 1) % result.shape[main_axis]] + place[main_axis + 1:]
    return result.at[tuple(place)].set(low).at[tuple(beside)].set(high)


def spiked(entries, own_key, source, target, blocks, factor):
    def block_of(position):
        return (jnp.arange(entries.shape[position]) // (entries.shape[position] // blocks)).reshape((-1,) + (1,) * (entries.ndim - 1 - position))

    near = jax.random.permutation(own_key, blocks)[block_of(target)]
    other_side = (block_of(target) + blocks // 2) % blocks
    return jnp.where((block_of(source) == near) | (block_of(source) == other_side), factor * entries, entries)


def level_of(stream_key, extent, cuts, smallest, high):
    factor_of, own = 1.0, jax.random.fold_in(stream_key, 6)
    for dim, blocks in cuts:
        steps = jnp.exp(jax.random.uniform(jax.random.fold_in(own, dim), (blocks,), jnp.float32, smallest / len(cuts), high / len(cuts)))
        factor_of = factor_of * jnp.repeat(steps, extent[dim] // blocks).reshape([-1 if axis == dim else 1 for axis in range(len(extent))])
    return factor_of


def noise(own_key, extent, spread, most, cuts=(), held_as=jnp.bfloat16):
    values = spread * jax.random.normal(own_key, extent, jnp.float32)
    if cuts:
        values = values * level_of(own_key, extent, cuts, -0.22, 0.18)
    return jnp.clip(values, -most, most).astype(held_as)


def gaussian_with(key, extent, width, reach, cuts, heavy, kind=jnp.bfloat16):
    values = width * jax.random.normal(key, extent, jnp.float32)
    if cuts:
        values = values * level_of(key, extent, cuts, -0.22, 0.18)
    return jnp.clip(spiked(values, jax.random.fold_in(key, 3), *heavy), -reach, reach).astype(kind)


def setup_inputs(seed: int = 0) -> dict:
    key_list = jax.random.split(jax.random.key(seed), 10)
    node_feats = noise(key_list[0], (H, NODES), 1.0, 6.0, ((0, 8), (1, 32)), jnp.float32)
    tiles = noise(key_list[1], (N_NODE * N_NODE, CAP, TB, TB), TB ** -0.5, 0.5, ((0, 32),), jnp.float32)
    send_col = draw_send_col(jax.random.fold_in(key_list[9], 71), 0)
    recv_row = draw_recv_row(jax.random.fold_in(key_list[9], 71), 0)
    degree = place_ends(jax.random.randint(key_list[4], (NODES,), 1, 9), jax.random.fold_in(key_list[4], 1), 1, 8).astype(jnp.int32)
    w_self = noise(key_list[5], (H, H), H ** -0.5, 0.375, (), jnp.float32)
    w_neigh = noise(key_list[6], (H, H), H ** -0.5, 0.375, (), jnp.float32)
    bias = noise(key_list[7], (H,), 0.5, 3.0, (), jnp.float32)
    cotangent = gaussian_with(key_list[8], (NODES, H), 1.0, 24.0, ((0, 256),), (0, 1, 256, 6.0), jnp.float32)
    return {"node_feats": node_feats, "tiles": tiles, "send_col": send_col, "recv_row": recv_row, "degree": degree, "w_self": w_self, "w_neigh": w_neigh, "bias": bias, "cotangent": cotangent}


def aggregate(node_feats, tiles, send_col, recv_row, degree):
    feat_blocks = node_feats.reshape(H, N_NODE, BLK_DEV, TB)
    sender_rows = recv_row.reshape(N_NODE, N_NODE, CAP).transpose(1, 0, 2)
    sender_cols = send_col.reshape(N_NODE, N_NODE, CAP)
    tile_grid = tiles.reshape(N_NODE, N_NODE, CAP, TB, TB)
    block_ids = jnp.arange(BLK_DEV, dtype=jnp.int32)

    def sender_step(totals, source):
        local = feat_blocks[:, source]
        col_onehot = (sender_cols[source][..., None] == block_ids).astype(jnp.float32)
        picked = jnp.einsum('dcb,hbj->dchj', col_onehot, local, precision=lax.Precision.HIGHEST)
        partial_value = jnp.einsum('dchj,dcij->dchi', picked, tile_grid[source], precision=lax.Precision.HIGHEST)
        row_onehot = (sender_rows[source][..., None] == block_ids).astype(jnp.float32)
        added = jnp.einsum('dchi,dcb->dhbi', partial_value, row_onehot, precision=lax.Precision.HIGHEST)
        return (totals + added, None)
    start_totals = jnp.zeros((N_NODE, H, BLK_DEV, TB), jnp.float32)
    totals, unused = lax.scan(sender_step, start_totals, jnp.arange(N_NODE, dtype=jnp.int32))
    summed = totals.transpose(1, 0, 2, 3).reshape(H, N_NODE * BLK_DEV * TB)
    return summed / degree.astype(jnp.float32)[None, :]

def reference(node_feats, tiles, send_col, recv_row, degree, w_self, w_neigh, bias, cotangent):

    def forward(feats, wself, wneigh, shift):
        neighbour = aggregate(feats, tiles, send_col, recv_row, degree)
        pre = jnp.dot(feats.T, wself, precision=lax.Precision.HIGHEST)
        pre = pre + jnp.dot(neighbour.T, wneigh, precision=lax.Precision.HIGHEST) + shift
        return jax.nn.silu(pre)
    activated, pullback = jax.vjp(forward, node_feats, w_self, w_neigh, bias)
    grads = pullback(cotangent)
    return (activated, grads[0], grads[1], grads[2], grads[3])
```

```python
import functools

import jax
import jax.numpy as jnp
from jax import lax
from jax.experimental import pallas as pl
from jax.experimental.pallas import tpu as pltpu
from jax.sharding import PartitionSpec as P

TB = 128
CAP = 4
NX = 4
NCH = 2
BF = jnp.bfloat16
F32 = jnp.float32
NN_DIMS = (((1,), (0,)), ((), ()))
NT_DIMS = (((1,), (1,)), ((), ()))


def split(x):
    hi = x.astype(BF)
    return hi, (x - hi.astype(F32)).astype(BF)


def dot(a, b, dims):
    return lax.dot_general(a, b, dims, preferred_element_type=F32)


def dot3(a, b, dims):
    return dot(a[0], b[0], dims) + dot(a[0], b[1], dims) + dot(a[1], b[0], dims)


def kernel(
    nn, nf, nx,
    feats, tiles, scol, rrow, deg, wself, wneigh, bias, cot,
    act_o, gf_o, gs_o, gn_o, gb_o,
    tv, fs, sb, rb, acc, xall, nsd, nall, wsh, wsl, wsth, wstl, wnh, wnl, wnth, wntl,
    cott, pret, gh, gl, act_v, gsd, grc, ssd, srv, bsd, brv, acc2, gf_v,
    r1s, r1r, r2s, r2r, r3s, r3r, r4s, r4r, outw, gb_v,
    tsem, xss, xrs, fss, frs, nss, nrs, gss, grs, sss, srs, bss, brs,
    r1ss, r1rs, r2ss, r2rs, r3ss, r3rs, r4ss, r4rs, r5ss, r5rs, osem,
):
    nz = nn // nx
    F = feats.shape[0]
    nblk = feats.shape[1] // TB
    Q = nblk // nf
    H = wself.shape[0]
    FC = F // NCH
    RZ = 2 * F // nz
    mf, mn = lax.axis_index("feat"), lax.axis_index("node")
    mx, mz = mn // nz, mn % nz

    def offset(j):
        dx = (j + 1) % nx
        t = j // nx
        dz = (nz // 2 + (1 - 2 * (t % 2)) * ((t + 1) // 2) + nz) % nz
        return dx, dz

    def target(j):
        dx, dz = offset(j)
        return ((mx + dx) % nx) * nz + (mz + dz) % nz

    def source(j):
        dx, dz = offset(j)
        return ((mx - dx + nx) % nx) * nz + (mz - dz + nz) % nz

    def remote(src, dst, ss, rs, **where):
        return pltpu.make_async_remote_copy(
            src_ref=src, dst_ref=dst, send_sem=ss, recv_sem=rs,
            device_id=where, device_id_type=pl.DeviceIdType.MESH,
        )

    barrier = pltpu.get_barrier_semaphore()

    @pl.loop(0, nn)
    def _(j):
        d = target(j)
        pltpu.make_async_copy(tiles.at[d], tv.at[d], tsem.at[d]).start()

    @pl.loop(1, nn)
    def _(k):
        pl.semaphore_signal(barrier, inc=1, device_id={"node": (mn + k) % nn},
                            device_id_type=pl.DeviceIdType.MESH)

    @pl.loop(1, nf)
    def _(k):
        pl.semaphore_signal(barrier, inc=1, device_id={"feat": (mf + k) % nf},
                            device_id_type=pl.DeviceIdType.MESH)

    for b in range(nblk):
        hi, lo = split(feats[:, b * TB:(b + 1) * TB])
        fs[b, :F] = hi
        fs[b, F:] = lo
    acc[...] = jnp.zeros_like(acc)
    acc2[...] = jnp.zeros_like(acc2)
    pl.semaphore_wait(barrier, nn - 1 + nf - 1)

    def x_copy(to):
        cols = pl.ds(pl.multiple_of(to * (Q * TB), Q * TB), Q * TB)
        rows = pl.ds(pl.multiple_of(mf * F, F), F)
        return remote(feats.at[:, cols], xall.at[rows, :], xss.at[to], xrs.at[mf], feat=to)

    @pl.loop(1, nf)
    def _(k):
        x_copy((mf + k) % nf).start()

    own_rows = pl.ds(pl.multiple_of(mf * F, F), F)
    xall[own_rows, :] = feats[:, pl.ds(pl.multiple_of(mf * (Q * TB), Q * TB), Q * TB)]

    def f_copy(h, d):
        return remote(sb.at[h, d], rb.at[h, mn], fss.at[h, d], frs.at[h, mn], node=d)

    def tile_forward(d):
        pltpu.make_async_copy(tiles.at[d], tv.at[d], tsem.at[d]).wait()
        for c in range(CAP):
            lhs = fs[scol[d, c]]
            th, tl = split(tv[d, c])
            o = dot(lhs, th, NT_DIMS)
            res = o[:F] + o[F:] + dot(lhs[:F], tl, NT_DIMS)
            for h in range(NCH):
                sb[h, d, c] = res[h * FC:(h + 1) * FC]

    @pl.loop(0, nn - 1)
    def _(j):
        d = target(j)
        tile_forward(d)
        f_copy(0, d).start()

    @pl.loop(0, (NCH - 1) * (nn - 1))
    def _(k):
        f_copy(1 + k // (nn - 1), target(k % (nn - 1))).start()

    tile_forward(mn)

    ws = wself[...]
    wsh[...], wsl[...] = split(ws)
    wsth[...], wstl[...] = split(ws.T)
    for h in range(NCH):
        rows = jnp.concatenate(
            [wneigh[f * F + h * FC:f * F + (h + 1) * FC, :] for f in range(nf)], axis=0)
        wnh[h], wnl[h] = split(rows)
        wnth[h], wntl[h] = split(rows.T)
    for q in range(Q):
        cott[:, q * TB:(q + 1) * TB] = cot[q * TB:(q + 1) * TB, :].T
    bias_t = jnp.broadcast_to(bias[...], (TB, H)).T

    @pl.loop(1, nf)
    def _(k):
        frm = (mf + nf - k) % nf
        rows = pl.ds(pl.multiple_of(frm * F, F), F)
        remote(xall.at[rows, :], xall.at[rows, :], xss.at[frm], xrs.at[frm], feat=frm).wait_recv()

    for q in range(Q):
        cols = slice(q * TB, (q + 1) * TB)
        pret[:, cols] = bias_t + dot3((wsth[...], wstl[...]), split(xall[:, cols]), NN_DIMS)

    def place(h, s, ref):
        vals = [ref[h, s, c] for c in range(CAP)]
        dest = [rrow[s, c] for c in range(CAP)]

        @pl.loop(0, nblk // 8)
        def _(g):
            for i in range(8):
                b = g * 8 + i
                a = acc[h, b]
                for c in range(CAP):
                    a = a + vals[c] * jnp.where(dest[c] == b, 1.0, 0.0)
                acc[h, b] = a

    def n_copy(h, to):
        return remote(nsd.at[h, to], nall.at[h, mf], nss.at[h, to], nrs.at[h, mf], feat=to)

    for h in range(NCH):
        place(h, mn, sb)

        @pl.loop(0, nn - 1)
        def _(j):
            s = source(j)
            remote(sb.at[h, s], rb.at[h, s], fss.at[h, s], frs.at[h, s], node=s).wait_recv()
            place(h, s, rb)

        @pl.loop(0, nf)
        def _(f):
            for q in range(Q):
                nsd[h, f, :, q * TB:(q + 1) * TB] = acc[h, f * Q + q]

        @pl.loop(1, nf)
        def _(k):
            n_copy(h, (mf + k) % nf).start()

        nall[h, mf] = nsd[h, mf]

    inv = [1.0 / deg[mf * Q + q].astype(F32) for q in range(Q)]
    for h in range(NCH):
        @pl.loop(1, nf)
        def _(k):
            frm = (mf + nf - k) % nf
            remote(nsd.at[h, frm], nall.at[h, frm], nss.at[h, frm], nrs.at[h, frm], feat=frm).wait_recv()

        for q in range(Q):
            cols = slice(q * TB, (q + 1) * TB)
            nb = nall[h, :, :, cols].reshape(nf * FC, TB) * inv[q]
            nall[h, :, :, cols] = nb.reshape(nf, FC, TB)
            pre = pret[:, cols] + dot3((wnth[h], wntl[h]), split(nb), NN_DIMS)
            pret[:, cols] = pre
            if h == NCH - 1:
                sig = 1.0 / (1.0 + jnp.exp(-pre))
                act_v[cols, :] = (pre * sig).T
                g = cott[:, cols] * (sig * (1.0 + pre * (1.0 - sig)))
                gh[:, cols], gl[:, cols] = split(g)
    act_copy = pltpu.make_async_copy(act_v, act_o, osem.at[0])
    act_copy.start()

    def g_copy(h, to):
        blocks = pl.ds(pl.multiple_of(mf * Q, Q), Q)
        return remote(gsd.at[h, to], grc[h].at[blocks], gss.at[h, to], grs.at[h, mf], feat=to)

    for h in range(NCH):
        for q in range(Q):
            cols = slice(q * TB, (q + 1) * TB)
            back = dot3((wnh[h], wnl[h]), (gh[:, cols], gl[:, cols]), NN_DIMS) * inv[q]
            for f in range(nf):
                gsd[h, f, q] = back[f * FC:(f + 1) * FC]

        @pl.loop(1, nf)
        def _(k):
            g_copy(h, (mf + k) % nf).start()

        for q in range(Q):
            grc[h][mf * Q + q] = gsd[h, mf, q]

    def r1_copy(to):
        return remote(r1s.at[to], r1r.at[mf], r1ss.at[to], r1rs.at[mf], feat=to)

    part_self = dot3(split(xall[...]), (gh[...], gl[...]), NT_DIMS)
    for f in range(nf):
        r1s[f, :F] = part_self[f * F:(f + 1) * F]
    for h in range(NCH):
        part = dot3(split(nall[h].reshape(nf * FC, Q * TB)), (gh[...], gl[...]), NT_DIMS)
        for f in range(nf):
            r1s[f, F + h * FC:F + (h + 1) * FC] = part[f * FC:(f + 1) * FC]
    ones = jnp.ones((16, Q * TB), BF)
    part_bias = (dot(ones, gh[...], NT_DIMS) + dot(ones, gl[...], NT_DIMS))[:8]
    for f in range(nf):
        r1s[f, 2 * F:] = part_bias

    def b_copy(h, d):
        return remote(bsd.at[h, d], brv.at[h, mn], bss.at[h, d], brs.at[h, mn], node=d)

    def pick(h, s, ref, at):
        for c in range(CAP):
            r = rrow[s, c]
            ref[h, at, c] = grc[h][jnp.maximum(r, 0)] * jnp.where(r >= 0, 1.0, 0.0)

    for h in range(NCH):
        @pl.loop(1, nf)
        def _(k):
            frm = (mf + nf - k) % nf
            blocks = pl.ds(pl.multiple_of(frm * Q, Q), Q)
            remote(gsd.at[h, frm], grc[h].at[blocks], gss.at[h, frm], grs.at[h, frm], feat=frm).wait_recv()

        @pl.loop(0, nn - 1)
        def _(j):
            d = target(j)
            pick(h, d, bsd, d)
            b_copy(h, d).start()

        pick(h, mn, brv, mn)

    @pl.loop(1, nf)
    def _(k):
        r1_copy((mf + k) % nf).start()

    r1r[mf] = r1s[mf]

    def s_copy(to):
        blocks = pl.ds(pl.multiple_of(mf * Q, Q), Q)
        return remote(ssd.at[to], srv.at[blocks], sss.at[to], srs.at[mf], feat=to)

    for q in range(Q):
        cols = slice(q * TB, (q + 1) * TB)
        back = dot3((wsh[...], wsl[...]), (gh[:, cols], gl[:, cols]), NN_DIMS)
        for f in range(nf):
            ssd[f, q] = back[f * F:(f + 1) * F]

    @pl.loop(1, nf)
    def _(k):
        s_copy((mf + k) % nf).start()

    for q in range(Q):
        srv[mf * Q + q] = ssd[mf, q]

    def tile_backward(d):
        outs = []
        for c in range(CAP):
            a = jnp.concatenate([brv[h, d, c] for h in range(NCH)], axis=0)
            ah, al = split(a)
            th, tl = split(tv[d, c])
            o = dot(jnp.concatenate([ah, al], axis=0), th, NN_DIMS)
            outs.append(o[:F] + o[F:] + dot(ah, tl, NN_DIMS))
        dest = [scol[d, c] for c in range(CAP)]

        @pl.loop(0, nblk // 8)
        def _(g):
            for i in range(8):
                b = g * 8 + i
                a = acc2[b]
                for c in range(CAP):
                    a = a + outs[c] * jnp.where(dest[c] == b, 1.0, 0.0)
                acc2[b] = a

    def backward_steps(start, stop):
        @pl.loop(start, stop)
        def _(j):
            d = source(j)
            for h in range(NCH):
                remote(bsd.at[h, d], brv.at[h, d], bss.at[h, d], brs.at[h, d], node=d).wait_recv()
            tile_backward(d)

    tile_backward(mn)

    @pl.loop(1, nf)
    def _(k):
        frm = (mf + nf - k) % nf
        remote(r1s.at[frm], r1r.at[frm], r1ss.at[frm], r1rs.at[frm], feat=frm).wait_recv()

    for z in range(nz):
        rows = slice(z * RZ, (z + 1) * RZ)
        r2s[z, :RZ] = sum((r1r[f, rows] for f in range(1, nf)), r1r[0, rows])
    bias_sum = sum((r1r[f, 2 * F:] for f in range(1, nf)), r1r[0, 2 * F:])
    for z in range(nz):
        r2s[z, RZ:] = bias_sum

    def r2_copy(z):
        return remote(r2s.at[z], r2r.at[mz], r2ss.at[z], r2rs.at[mz], node=mx * nz + z)

    @pl.loop(1, nz)
    def _(k):
        r2_copy((mz + k) % nz).start()

    r2r[mz] = r2s[mz]
    step = (nn - 1) // 4
    backward_steps(0, step)

    @pl.loop(1, nz)
    def _(k):
        z = (mz + nz - k) % nz
        remote(r2s.at[z], r2r.at[z], r2ss.at[z], r2rs.at[z], node=mx * nz + z).wait_recv()

    r3s[...] = sum((r2r[z] for z in range(1, nz)), r2r[0])

    def r3_copy(x):
        return remote(r3s, r3r.at[mx], r3ss.at[x], r3rs.at[mx], node=x * nz + mz)

    @pl.loop(1, nx)
    def _(k):
        r3_copy((mx + k) % nx).start()

    r3r[mx] = r3s[...]
    backward_steps(step, 2 * step)

    @pl.loop(1, nx)
    def _(k):
        x = (mx + nx - k) % nx
        remote(r3s, r3r.at[x], r3ss.at[x], r3rs.at[x], node=x * nz + mz).wait_recv()

    total = sum((r3r[x] for x in range(1, nx)), r3r[0])
    r4s[...] = total[:RZ]
    gb_v[...] = total[RZ:RZ + 1]

    def r4_copy(z):
        return remote(r4s, r4r.at[mz], r4ss.at[z], r4rs.at[mz], node=mx * nz + z)

    @pl.loop(1, nz)
    def _(k):
        r4_copy((mz + k) % nz).start()

    r4r[mz] = r4s[...]
    backward_steps(2 * step, 3 * step)

    @pl.loop(1, nz)
    def _(k):
        z = (mz + nz - k) % nz
        remote(r4s, r4r.at[z], r4ss.at[z], r4rs.at[z], node=mx * nz + z).wait_recv()

    def r5_copy(i, to):
        part = r4r.at[pl.ds(i * (nz // 2), nz // 2)]
        rows = pl.ds(pl.multiple_of(mf * nz // 2, nz // 2), nz // 2)
        return remote(part, outw.at[i, rows], r5ss.at[i, to], r5rs.at[i, mf], feat=to)

    for i in range(2):
        @pl.loop(1, nf)
        def _(k):
            r5_copy(i, (mf + k) % nf).start()

        for z in range(nz // 2):
            outw[i, mf * (nz // 2) + z] = r4r[i * (nz // 2) + z]
    backward_steps(3 * step, nn - 1)

    @pl.loop(1, nf)
    def _(k):
        frm = (mf + nf - k) % nf
        blocks = pl.ds(pl.multiple_of(frm * Q, Q), Q)
        remote(ssd.at[frm], srv.at[blocks], sss.at[frm], srs.at[frm], feat=frm).wait_recv()

    for b in range(nblk):
        gf_v[:, b * TB:(b + 1) * TB] = srv[b] + acc2[b]
    gf_copy = pltpu.make_async_copy(gf_v, gf_o, osem.at[1])
    gf_copy.start()
    for i in range(2):
        @pl.loop(1, nf)
        def _(k):
            frm = (mf + nf - k) % nf
            part = r4r.at[pl.ds(i * (nz // 2), nz // 2)]
            rows = pl.ds(pl.multiple_of(frm * nz // 2, nz // 2), nz // 2)
            remote(part, outw.at[i, rows], r5ss.at[i, frm], r5rs.at[i, frm], feat=frm).wait_recv()
    tail = [
        pltpu.make_async_copy(outw.at[0], gs_o, osem.at[2]),
        pltpu.make_async_copy(outw.at[1], gn_o, osem.at[3]),
        pltpu.make_async_copy(gb_v, gb_o, osem.at[4]),
    ]
    for copy in tail:
        copy.start()

    @pl.loop(1, nf)
    def _(k):
        to = (mf + k) % nf
        x_copy(to).wait_send()
        r1_copy(to).wait_send()
        s_copy(to).wait_send()
        for h in range(NCH):
            n_copy(h, to).wait_send()
            g_copy(h, to).wait_send()
        for i in range(2):
            r5_copy(i, to).wait_send()

    @pl.loop(1, nz)
    def _(k):
        z = (mz + k) % nz
        r2_copy(z).wait_send()
        r4_copy(z).wait_send()

    @pl.loop(1, nx)
    def _(k):
        r3_copy((mx + k) % nx).wait_send()

    @pl.loop(0, nn - 1)
    def _(j):
        d = target(j)
        for h in range(NCH):
            f_copy(h, d).wait_send()
            b_copy(h, d).wait_send()

    act_copy.wait()
    gf_copy.wait()
    for copy in tail:
        copy.wait()


def shards(nn, nf, nx, node_feats, tiles, send_col, recv_row, degree, w_self, w_neigh, bias, cotangent):
    F, owned = node_feats.shape
    nz = nn // nx
    nblk = owned // TB
    Q = nblk // nf
    H = w_self.shape[0]
    FC = F // NCH
    RZ = 2 * F // nz
    cols = Q * TB
    vmem, anyw, smem = (pl.BlockSpec(memory_space=s) for s in (pltpu.VMEM, pl.ANY, pltpu.SMEM))
    V, D = pltpu.VMEM, pltpu.SemaphoreType.DMA
    scratch = [
        V((nn, CAP, TB, TB), F32),
        V((nblk, 2 * F, TB), BF),
        V((NCH, nn, CAP, FC, TB), F32),
        V((NCH, nn, CAP, FC, TB), F32),
        V((NCH, nblk, FC, TB), F32),
        V((H, cols), F32),
        V((NCH, nf, FC, cols), F32),
        V((NCH, nf, FC, cols), F32),
        V((H, H), BF), V((H, H), BF), V((H, H), BF), V((H, H), BF),
        V((NCH, H // NCH, H), BF), V((NCH, H // NCH, H), BF),
        V((NCH, H, H // NCH), BF), V((NCH, H, H // NCH), BF),
        V((H, cols), F32), V((H, cols), F32),
        V((H, cols), BF), V((H, cols), BF),
        V((cols, H), F32),
        V((NCH, nf, Q, FC, TB), F32),
        [V((nblk, FC, TB), F32) for _ in range(NCH)],
        V((nf, Q, F, TB), F32),
        V((nblk, F, TB), F32),
        V((NCH, nn, CAP, FC, TB), F32),
        V((NCH, nn, CAP, FC, TB), F32),
        V((nblk, F, TB), F32),
        V((F, owned), F32),
        V((nf, 2 * F + 8, H), F32), V((nf, 2 * F + 8, H), F32),
        V((nz, RZ + 8, H), F32), V((nz, RZ + 8, H), F32),
        V((RZ + 8, H), F32), V((nx, RZ + 8, H), F32),
        V((RZ, H), F32), V((nz, RZ, H), F32),
        V((2, nf * nz // 2, RZ, H), F32),
        V((1, H), F32),
        D((nn,)),
        D((nf,)), D((nf,)),
        D((NCH, nn)), D((NCH, nn)),
        D((NCH, nf)), D((NCH, nf)),
        D((NCH, nf)), D((NCH, nf)),
        D((nf,)), D((nf,)),
        D((NCH, nn)), D((NCH, nn)),
        D((nf,)), D((nf,)),
        D((nz,)), D((nz,)),
        D((nx,)), D((nx,)),
        D((nz,)), D((nz,)),
        D((2, nf)), D((2, nf)),
        D((5,)),
    ]
    act, gf, gs, gn, gb = pl.pallas_call(
        functools.partial(kernel, nn, nf, nx),
        out_shape=[
            jax.ShapeDtypeStruct((cols, H), F32),
            jax.ShapeDtypeStruct((F, owned), F32),
            jax.ShapeDtypeStruct((nf * nz // 2, RZ, H), F32),
            jax.ShapeDtypeStruct((nf * nz // 2, RZ, H), F32),
            jax.ShapeDtypeStruct((1, H), F32),
        ],
        in_specs=[vmem, anyw, smem, smem, vmem, vmem, vmem, vmem, vmem],
        out_specs=[anyw] * 5,
        scratch_shapes=scratch,
        compiler_params=pltpu.CompilerParams(
            collective_id=0, has_side_effects=True, vmem_limit_bytes=50 * 1024 * 1024
        ),
    )(
        node_feats, tiles, send_col, recv_row, degree.reshape(nblk, 1, TB),
        w_self, w_neigh, bias.reshape(1, H), cotangent,
    )
    return act, gf, gs.reshape(H, H), gn.reshape(H, H), gb.reshape(H)


def solution(mesh):
    return jax.shard_map(
        functools.partial(shards, mesh.shape["node"], mesh.shape["feat"], NX),
        mesh=mesh,
        in_specs=(
            P("feat", "node"),
            P("node", None, None, None),
            P("node", None),
            P("node", None),
            P("node"),
            P(),
            P(),
            P(),
            P(("node", "feat"), None),
        ),
        out_specs=(P(("node", "feat"), None), P("feat", "node"), P(), P(), P()),
        check_vma=False,
    )
```

```python
import functools

import jax
import jax.numpy as jnp
from jax import lax
from jax.experimental import pallas as pl
from jax.experimental.pallas import tpu as pltpu
from jax.sharding import PartitionSpec as P

TB = 128
CAP = 4
NX = 4
NCH = 2
BF = jnp.bfloat16
F32 = jnp.float32
NN_DIMS = (((1,), (0,)), ((), ()))
NT_DIMS = (((1,), (1,)), ((), ()))
MESH = pl.DeviceIdType.MESH


def shift(t):
    return (2 * (t % 2) - 1) * ((t + 1) // 2)


def split(x):
    hi = x.astype(BF)
    return hi, (x - hi.astype(F32)).astype(BF)


def dot(a, b, dims):
    return lax.dot_general(a, b, dims, preferred_element_type=F32)


def dot3(a, b, dims):
    return dot(a[0], b[0], dims) + dot(a[0], b[1], dims) + dot(a[1], b[0], dims)


def total(ref, n):
    return sum((ref[i] for i in range(1, n)), ref[0])


def kernel(
    nn, nf, nx,
    feats_a, tiles, scol, rrow, deg_a, wself_a, wneigh_a, bias_a, cot_a,
    act_o, gf_o, gs_o, gn_o, gb_o,
    feats, deg, wself, wneigh, bias, cot,
    tv, fs, sb, rb, acc, dr, xall, nsd, nall, wsh, wsl, wsth, wstl, wnh, wnl, wnth, wntl,
    cott, pret, gh, gl, act_v, gsd, grc, gnb, ssd, srv, bsd, brv, acc2, gf_v,
    r1s, r1r, r2s, r2r, r3s, r3r, r4s, r4r, outw, gb_v, rtab,
    isem, tsem, xss, xrs, mss, mrs, fss, frs, dss, drs, nss, nrs, gss, grs, ess, ers, sss, srs, bss, brs,
    r1ss, r1rs, r2ss, r2rs, r3ss, r3rs, r4ss, r4rs, r5ss, r5rs, osem,
):
    nz = nn // nx
    F = feats.shape[0]
    nblk = feats.shape[1] // TB
    Q = nblk // nf
    H = wself.shape[0]
    FC = F // NCH
    RX = 2 * F // nx
    mf, mn = lax.axis_index("feat"), lax.axis_index("node")
    mx, mz = mn // nz, mn % nz

    def xat(dx):
        return (mx + dx + nx) % nx

    def zat(dz):
        return (mz + dz + nz) % nz

    def remote(src, dst, ss, rs, **where):
        return pltpu.make_async_remote_copy(
            src_ref=src, dst_ref=dst, send_sem=ss, recv_sem=rs, device_id=where, device_id_type=MESH)

    barrier = pltpu.get_barrier_semaphore()

    @pl.loop(1, 7 * nx)
    def _(j):
        node = xat(j // 7) * nz + zat((j % 7 + 3) % 7 - 3)
        pl.semaphore_signal(barrier, inc=1, device_id={"node": node}, device_id_type=MESH)

    pl.semaphore_signal(barrier, inc=1, device_id={"node": mx * nz + zat(4)}, device_id_type=MESH)

    @pl.loop(1, nf)
    def _(k):
        pl.semaphore_signal(barrier, inc=1, device_id={"feat": (mf + k) % nf}, device_id_type=MESH)

    loads = [
        pltpu.make_async_copy(src, dst, isem.at[i])
        for i, (src, dst) in enumerate([
            (feats_a, feats), (wself_a, wself), (wneigh_a, wneigh), (cot_a, cot), (deg_a, deg), (bias_a, bias)])
    ]
    loads[0].start()

    def owner(x, g):
        return x * nz + zat(shift(g))

    def tile_load(x, g):
        d = owner(x, g)
        return pltpu.make_async_copy(tiles.at[d], tv.at[d], tsem.at[d])

    def order(j):
        return xat(j + 1), ((j // nx) + 2) % 4 + 1

    for g in range(3):
        tile_load(mx, g).start()

    @pl.loop(0, nx)
    def _(j):
        tile_load(xat(j + 1), 7).start()

    @pl.loop(0, 4 * nx)
    def _(j):
        x, t = order(j)
        tile_load(x, t + 2).start()

    @pl.loop(0, nx - 1)
    def _(j):
        for g in range(3):
            tile_load(xat(j + 1), g).start()

    for copy in loads[1:]:
        copy.start()
    loads[0].wait()
    for b in range(nblk):
        hi, lo = split(feats[:, b * TB:(b + 1) * TB])
        fs[b, :F] = hi
        fs[b, F:] = lo
    acc[...] = jnp.zeros_like(acc)
    acc2[...] = jnp.zeros_like(acc2)

    def tile_forward(x, g):
        d = owner(x, g)
        tile_load(x, g).wait()
        for c in range(CAP):
            lhs = fs[scol[c, d]]
            th, tl = split(tv[d, c])
            o = dot(lhs, th, NT_DIMS)
            res = o[:F] + o[F:] + dot(lhs[:F], tl, NT_DIMS)
            for h in range(NCH):
                sb[h, x, 4 * g + c] = res[h * FC:(h + 1) * FC]

    for g in range(3):
        tile_forward(mx, g)
    pl.semaphore_wait(barrier, 7 * nx - 1 + 1 + nf - 1)

    def m_copy(i):
        return remote(rrow, rtab.at[i], mss.at[i], mrs.at[i], node=mx * nz + zat(2 * i - 1))

    for i in range(2):
        m_copy(i).start()

    def x_copy(to):
        cols = pl.ds(pl.multiple_of(to * (Q * TB), Q * TB), Q * TB)
        rows = pl.ds(pl.multiple_of(mf * F, F), F)
        return remote(feats.at[:, cols], xall.at[rows, :], xss.at[to], xrs.at[mf], feat=to)

    @pl.loop(1, nf)
    def _(k):
        x_copy((mf + k) % nf).start()

    own_rows = pl.ds(pl.multiple_of(mf * F, F), F)
    xall[own_rows, :] = feats[:, pl.ds(pl.multiple_of(mf * (Q * TB), Q * TB), Q * TB)]

    def place(t):
        if not isinstance(t, int):
            return pl.ds(4 * t + 8, 4)
        return pl.ds(0, 12) if t == 0 else pl.ds(4 * t + 8, 4) if t < 5 else pl.ds(18 + 2 * t, 2)

    def f_copy(h, x, t):
        at = place(t)
        return remote(sb.at[h, x, at], rb.at[h, mx, at], fss.at[h, x, t], frs.at[h, mx, t],
                      node=x * nz + zat(shift(t)))

    def b_copy(h, x, t):
        at = place(t)
        return remote(bsd.at[h, x, at], brv.at[h, mx, at], bss.at[h, x, t], brs.at[h, mx, t],
                      node=x * nz + zat(-shift(t)))

    def f_arrived(h, x, t):
        at = place(t)
        remote(sb.at[h, x, at], rb.at[h, x, at], fss.at[h, x, t], frs.at[h, x, t],
               node=x * nz + zat(-shift(t))).wait_recv()

    def b_arrived(h, x, t):
        at = place(t)
        remote(bsd.at[h, x, at], brv.at[h, x, at], bss.at[h, x, t], brs.at[h, x, t],
               node=x * nz + zat(shift(t))).wait_recv()

    @pl.loop(0, nx)
    def _(j):
        x = xat(j + 1)
        tile_forward(x, 7)
        f_copy(0, x, 5).start()
        f_copy(0, x, 6).start()

    @pl.loop(0, 4 * nx)
    def _(j):
        x, t = order(j)
        tile_forward(x, t + 2)
        f_copy(0, x, t).start()

    @pl.loop(0, nx - 1)
    def _(j):
        x = xat(j + 1)
        for g in range(3):
            tile_forward(x, g)
        f_copy(0, x, 0).start()

    for h in range(1, NCH):
        @pl.loop(0, nx)
        def _(j):
            f_copy(h, xat(j + 1), 5).start()
            f_copy(h, xat(j + 1), 6).start()

        @pl.loop(0, 4 * nx)
        def _(j):
            x, t = order(j)
            f_copy(h, x, t).start()

        @pl.loop(0, nx - 1)
        def _(j):
            f_copy(h, xat(j + 1), 0).start()

    for copy in loads[1:]:
        copy.wait()
    ws = wself[...]
    wsh[...], wsl[...] = split(ws)
    wsth[...], wstl[...] = split(ws.T)
    for h in range(NCH):
        rows = jnp.concatenate(
            [wneigh[f * F + h * FC:f * F + (h + 1) * FC, :] for f in range(nf)], axis=0)
        wnh[h], wnl[h] = split(rows)
        wnth[h], wntl[h] = split(rows.T)
    for q in range(Q):
        cott[:, q * TB:(q + 1) * TB] = cot[q * TB:(q + 1) * TB, :].T
    bias_t = jnp.broadcast_to(bias[...], (TB, H)).T

    @pl.loop(1, nf)
    def _(k):
        frm = (mf + nf - k) % nf
        rows = pl.ds(pl.multiple_of(frm * F, F), F)
        remote(xall.at[rows, :], xall.at[rows, :], xss.at[frm], xrs.at[frm], feat=frm).wait_recv()

    for q in range(Q):
        cols = slice(q * TB, (q + 1) * TB)
        pret[:, cols] = bias_t + dot3((wsth[...], wstl[...]), split(xall[:, cols]), NN_DIMS)
    for i in range(2):
        remote(rrow, rtab.at[i], mss.at[i], mrs.at[i], node=mx * nz + zat(1 - 2 * i)).wait_recv()

    def add(h, role, vals, dest):
        @pl.loop(0, nblk // 8)
        def _(k):
            for i in range(8):
                b = k * 8 + i
                a = acc[role, h, b]
                for v, r in zip(vals, dest):
                    a = a + v * jnp.where(r == b, 1.0, 0.0)
                acc[role, h, b] = a

    def add_plane(h, x, ref):
        s = x * nz + mz
        for g in range(3):
            rows = [rrow[c, s] if g == 0 else rtab[g - 1, c, s] for c in range(CAP)]
            add(h, g, [ref[h, x, 4 * g + c] for c in range(CAP)], rows)

    def d_copy(h, i):
        return remote(acc.at[1 + i, h], dr.at[h, i], dss.at[h, i], drs.at[h, i],
                      node=mx * nz + zat(1 - 2 * i))

    for h in range(NCH):
        add_plane(h, mx, sb)

        @pl.loop(0, nx)
        def _(j):
            x = xat(-1 - j)
            for i in range(2):
                f_arrived(h, x, 5 + i)
                s = x * nz + zat(-shift(5 + i))
                add(h, 1 + i, [rb[h, x, 28 + 2 * i + c] for c in range(2)],
                    [rtab[i, 2 * i + c, s] for c in range(2)])

        @pl.loop(0, 4 * nx)
        def _(j):
            t = order(j)[1]
            x = xat(-1 - j % nx)
            f_arrived(h, x, t)
            s = x * nz + zat(-shift(t))
            side = 1 - t % 2
            add(h, 1 + side, [rb[h, x, 4 * t + 8 + c] for c in range(CAP)],
                [rtab[side, c, s] for c in range(CAP)])

        @pl.loop(0, nx - 1)
        def _(j):
            x = xat(-1 - j)
            f_arrived(h, x, 0)
            add_plane(h, x, rb)

        for i in range(2):
            d_copy(h, i).start()

    def n_copy(h, to):
        return remote(nsd.at[h, to], nall.at[h, mf], nss.at[h, to], nrs.at[h, mf], feat=to)

    for h in range(NCH):
        for i in range(2):
            remote(acc.at[1 + i, h], dr.at[h, i], dss.at[h, i], drs.at[h, i],
                   node=mx * nz + zat(2 * i - 1)).wait_recv()

        @pl.loop(0, nf)
        def _(f):
            for q in range(Q):
                b = f * Q + q
                nsd[h, f, :, q * TB:(q + 1) * TB] = acc[0, h, b] + dr[h, 0, b] + dr[h, 1, b]

        @pl.loop(1, nf)
        def _(k):
            n_copy(h, (mf + k) % nf).start()

        nall[h, mf] = nsd[h, mf]

    inv = [1.0 / deg[mf * Q + q].astype(F32) for q in range(Q)]
    for h in range(NCH):
        @pl.loop(1, nf)
        def _(k):
            frm = (mf + nf - k) % nf
            remote(nsd.at[h, frm], nall.at[h, frm], nss.at[h, frm], nrs.at[h, frm], feat=frm).wait_recv()

        for q in range(Q):
            cols = slice(q * TB, (q + 1) * TB)
            nb = nall[h, :, :, cols].reshape(nf * FC, TB) * inv[q]
            nall[h, :, :, cols] = nb.reshape(nf, FC, TB)
            pre = pret[:, cols] + dot3((wnth[h], wntl[h]), split(nb), NN_DIMS)
            pret[:, cols] = pre
            if h == NCH - 1:
                sig = 1.0 / (1.0 + jnp.exp(-pre))
                act_v[cols, :] = (pre * sig).T
                g = cott[:, cols] * (sig * (1.0 + pre * (1.0 - sig)))
                gh[:, cols], gl[:, cols] = split(g)
    act_copy = pltpu.make_async_copy(act_v, act_o, osem.at[0])
    act_copy.start()

    def g_copy(h, to):
        blocks = pl.ds(pl.multiple_of(mf * Q, Q), Q)
        return remote(gsd.at[h, to], grc[h].at[blocks], gss.at[h, to], grs.at[h, mf], feat=to)

    for h in range(NCH):
        for q in range(Q):
            cols = slice(q * TB, (q + 1) * TB)
            back = dot3((wnh[h], wnl[h]), (gh[:, cols], gl[:, cols]), NN_DIMS) * inv[q]
            for f in range(nf):
                gsd[h, f, q] = back[f * FC:(f + 1) * FC]

        @pl.loop(1, nf)
        def _(k):
            g_copy(h, (mf + k) % nf).start()

        for q in range(Q):
            grc[h][mf * Q + q] = gsd[h, mf, q]

    def r1_copy(to):
        return remote(r1s.at[to], r1r.at[mf], r1ss.at[to], r1rs.at[mf], feat=to)

    part_self = dot3(split(xall[...]), (gh[...], gl[...]), NT_DIMS)
    for f in range(nf):
        r1s[f, :F] = part_self[f * F:(f + 1) * F]
    for h in range(NCH):
        part = dot3(split(nall[h].reshape(nf * FC, Q * TB)), (gh[...], gl[...]), NT_DIMS)
        for f in range(nf):
            r1s[f, F + h * FC:F + (h + 1) * FC] = part[f * FC:(f + 1) * FC]
    ones = jnp.ones((16, Q * TB), BF)
    part_bias = (dot(ones, gh[...], NT_DIMS) + dot(ones, gl[...], NT_DIMS))[:8]
    for f in range(nf):
        r1s[f, 2 * F:] = part_bias

    @pl.loop(1, nf)
    def _(k):
        r1_copy((mf + k) % nf).start()

    r1r[mf] = r1s[mf]

    def e_copy(h, i):
        return remote(grc[h], gnb[h][i], ess.at[h, i], ers.at[h, i], node=mx * nz + zat(2 * i - 1))

    for h in range(NCH):
        @pl.loop(1, nf)
        def _(k):
            frm = (mf + nf - k) % nf
            blocks = pl.ds(pl.multiple_of(frm * Q, Q), Q)
            remote(gsd.at[h, frm], grc[h].at[blocks], gss.at[h, frm], grs.at[h, frm], feat=frm).wait_recv()

        for i in range(2):
            e_copy(h, i).start()

    def s_copy(to):
        blocks = pl.ds(pl.multiple_of(mf * Q, Q), Q)
        return remote(ssd.at[to], srv.at[blocks], sss.at[to], srs.at[mf], feat=to)

    for q in range(Q):
        cols = slice(q * TB, (q + 1) * TB)
        back = dot3((wsh[...], wsl[...]), (gh[:, cols], gl[:, cols]), NN_DIMS)
        for f in range(nf):
            ssd[f, q] = back[f * F:(f + 1) * F]

    @pl.loop(1, nf)
    def _(k):
        s_copy((mf + k) % nf).start()

    for q in range(Q):
        srv[mf * Q + q] = ssd[mf, q]

    def pick(src, r):
        return src[jnp.maximum(r, 0)] * jnp.where(r >= 0, 1.0, 0.0)

    def pick_plane(h, x, ref):
        s = x * nz + mz
        for g in range(3):
            src = grc[h] if g == 0 else gnb[h][g - 1]
            for c in range(CAP):
                ref[h, x, 4 * g + c] = pick(src, rrow[c, s] if g == 0 else rtab[g - 1, c, s])

    def pick_all(h):
        for i in range(2):
            remote(grc[h], gnb[h][i], ess.at[h, i], ers.at[h, i], node=mx * nz + zat(1 - 2 * i)).wait_recv()

        @pl.loop(0, nx)
        def _(j):
            x = xat(j + 1)
            for i in range(2):
                s = x * nz + zat(-shift(5 + i))
                for c in range(2):
                    bsd[h, x, 28 + 2 * i + c] = pick(gnb[h][i], rtab[i, 2 * i + c, s])
                b_copy(h, x, 5 + i).start()

        for t in (3, 4, 1, 2):
            @pl.loop(0, nx)
            def _(j):
                x = xat(j + 1)
                s = x * nz + zat(-shift(t))
                side = 1 - t % 2
                for c in range(CAP):
                    bsd[h, x, 4 * t + 8 + c] = pick(gnb[h][side], rtab[side, c, s])
                b_copy(h, x, t).start()

        @pl.loop(0, nx - 1)
        def _(j):
            x = xat(j + 1)
            pick_plane(h, x, bsd)
            b_copy(h, x, 0).start()

        pick_plane(h, mx, brv)

    for h in range(NCH - 1):
        pick_all(h)

    @pl.loop(1, nf)
    def _(k):
        frm = (mf + nf - k) % nf
        remote(r1s.at[frm], r1r.at[frm], r1ss.at[frm], r1rs.at[frm], feat=frm).wait_recv()

    bias_sum = sum((r1r[f, 2 * F:] for f in range(1, nf)), r1r[0, 2 * F:])
    for x in range(nx):
        rows = slice(x * RX, (x + 1) * RX)
        r2s[x, :RX] = sum((r1r[f, rows] for f in range(1, nf)), r1r[0, rows])
        r2s[x, RX:] = bias_sum

    def r2_copy(x):
        return remote(r2s.at[x], r2r.at[mx], r2ss.at[x], r2rs.at[mx], node=x * nz + mz)

    @pl.loop(1, nx)
    def _(k):
        r2_copy(xat(k)).start()

    r2r[mx] = r2s[mx]

    @pl.loop(1, nx)
    def _(k):
        x = xat(-k)
        remote(r2s.at[x], r2r.at[x], r2ss.at[x], r2rs.at[x], node=x * nz + mz).wait_recv()

    r3s[...] = total(r2r, nx)

    def r3_copy(z):
        return remote(r3s, r3r.at[mz], r3ss.at[z], r3rs.at[mz], node=mx * nz + z)

    @pl.loop(1, nz)
    def _(k):
        r3_copy(zat(k)).start()

    r3r[mz] = r3s[...]
    pick_all(NCH - 1)

    def tile_backward(x, g):
        d = owner(x, g)
        outs = []
        for c in range(CAP):
            a = jnp.concatenate([brv[h, x, 4 * g + c] for h in range(NCH)], axis=0)
            ah, al = split(a)
            th, tl = split(tv[d, c])
            o = dot(jnp.concatenate([ah, al], axis=0), th, NN_DIMS)
            outs.append(o[:F] + o[F:] + dot(ah, tl, NN_DIMS))
        dest = [scol[c, d] for c in range(CAP)]

        @pl.loop(0, nblk // 8)
        def _(k):
            for i in range(8):
                b = k * 8 + i
                a = acc2[b]
                for c in range(CAP):
                    a = a + outs[c] * jnp.where(dest[c] == b, 1.0, 0.0)
                acc2[b] = a

    for g in range(3):
        tile_backward(mx, g)

    @pl.loop(1, nz)
    def _(k):
        z = zat(-k)
        remote(r3s, r3r.at[z], r3ss.at[z], r3rs.at[z], node=mx * nz + z).wait_recv()

    grads = total(r3r, nz)
    r4s[...] = grads[:RX]
    gb_v[...] = grads[RX:RX + 1]

    def r4_copy(x):
        return remote(r4s, r4r.at[mx], r4ss.at[x], r4rs.at[mx], node=x * nz + mz)

    @pl.loop(1, nx)
    def _(k):
        r4_copy(xat(k)).start()

    r4r[mx] = r4s[...]

    @pl.loop(1, nf)
    def _(k):
        to = (mf + k) % nf
        x_copy(to).wait_send()
        r1_copy(to).wait_send()
        s_copy(to).wait_send()
        for h in range(NCH):
            n_copy(h, to).wait_send()
            g_copy(h, to).wait_send()

    for h in range(NCH):
        @pl.loop(0, nx)
        def _(j):
            f_copy(h, xat(j + 1), 5).wait_send()
            f_copy(h, xat(j + 1), 6).wait_send()

        @pl.loop(0, 4 * nx)
        def _(j):
            x, t = order(j)
            f_copy(h, x, t).wait_send()

        @pl.loop(0, nx - 1)
        def _(j):
            f_copy(h, xat(j + 1), 0).wait_send()

        for i in range(2):
            d_copy(h, i).wait_send()
            e_copy(h, i).wait_send()
    for i in range(2):
        m_copy(i).wait_send()

    @pl.loop(1, nx)
    def _(k):
        r2_copy(xat(k)).wait_send()

    @pl.loop(1, nz)
    def _(k):
        r3_copy(zat(k)).wait_send()

    @pl.loop(0, nx)
    def _(j):
        x = xat(-1 - j)
        for h in range(NCH):
            b_arrived(h, x, 5)
            b_arrived(h, x, 6)
        tile_backward(x, 7)

    def r5_copy(i, to):
        part = r4r.at[pl.ds(i * (nx // 2), nx // 2)]
        rows = pl.ds(pl.multiple_of(mf * (nx // 2), nx // 2), nx // 2)
        return remote(part, outw.at[i, rows], r5ss.at[i, to], r5rs.at[i, mf], feat=to)

    def middle(start, stop):
        @pl.loop(start, stop)
        def _(j):
            t = order(j)[1]
            x = xat(-1 - j % nx)
            for h in range(NCH):
                b_arrived(h, x, t)
            tile_backward(x, t + 2)

    middle(0, 2 * nx)

    @pl.loop(1, nx)
    def _(k):
        x = xat(-k)
        remote(r4s, r4r.at[x], r4ss.at[x], r4rs.at[x], node=x * nz + mz).wait_recv()

    for i in range(2):
        @pl.loop(1, nf)
        def _(k):
            r5_copy(i, (mf + k) % nf).start()

        for x in range(nx // 2):
            outw[i, mf * (nx // 2) + x] = r4r[i * (nx // 2) + x]
    middle(2 * nx, 4 * nx)

    @pl.loop(0, nx - 1)
    def _(j):
        x = xat(-1 - j)
        for h in range(NCH):
            b_arrived(h, x, 0)
        for g in range(3):
            tile_backward(x, g)

    @pl.loop(1, nf)
    def _(k):
        frm = (mf + nf - k) % nf
        blocks = pl.ds(pl.multiple_of(frm * Q, Q), Q)
        remote(ssd.at[frm], srv.at[blocks], sss.at[frm], srs.at[frm], feat=frm).wait_recv()

    for b in range(nblk):
        gf_v[:, b * TB:(b + 1) * TB] = srv[b] + acc2[b]
    gf_copy = pltpu.make_async_copy(gf_v, gf_o, osem.at[1])
    gf_copy.start()
    for i in range(2):
        @pl.loop(1, nf)
        def _(k):
            frm = (mf + nf - k) % nf
            part = r4r.at[pl.ds(i * (nx // 2), nx // 2)]
            rows = pl.ds(pl.multiple_of(frm * (nx // 2), nx // 2), nx // 2)
            remote(part, outw.at[i, rows], r5ss.at[i, frm], r5rs.at[i, frm], feat=frm).wait_recv()
    tail = [
        pltpu.make_async_copy(outw.at[0], gs_o, osem.at[2]),
        pltpu.make_async_copy(outw.at[1], gn_o, osem.at[3]),
        pltpu.make_async_copy(gb_v, gb_o, osem.at[4]),
    ]
    for copy in tail:
        copy.start()

    @pl.loop(1, nf)
    def _(k):
        for i in range(2):
            r5_copy(i, (mf + k) % nf).wait_send()

    @pl.loop(1, nx)
    def _(k):
        r4_copy(xat(k)).wait_send()

    for h in range(NCH):
        @pl.loop(0, nx)
        def _(j):
            b_copy(h, xat(j + 1), 5).wait_send()
            b_copy(h, xat(j + 1), 6).wait_send()

        @pl.loop(0, 4 * nx)
        def _(j):
            x, t = order(j)
            b_copy(h, x, t).wait_send()

        @pl.loop(0, nx - 1)
        def _(j):
            b_copy(h, xat(j + 1), 0).wait_send()

    act_copy.wait()
    gf_copy.wait()
    for copy in tail:
        copy.wait()


def hand_over(*refs):
    n = (len(refs) - 1) // 3
    sem = refs[-1]
    takes = [pltpu.make_async_copy(refs[i], refs[2 * n + i], sem.at[0, i]) for i in range(n)]
    gives = [pltpu.make_async_copy(refs[2 * n + i], refs[n + i], sem.at[1, i]) for i in range(n)]
    for take in takes:
        take.start()
    for take, give in zip(takes, gives):
        take.wait()
        give.start()
    for give in gives:
        give.wait()


def shards(nn, nf, nx, node_feats, tiles, send_col, recv_row, degree, w_self, w_neigh, bias, cotangent):
    F, owned = node_feats.shape
    nz = nn // nx
    nblk = owned // TB
    Q = nblk // nf
    H = w_self.shape[0]
    FC = F // NCH
    RX = 2 * F // nx
    cols = Q * TB
    slots = nz * CAP
    anyw, smem = pl.BlockSpec(memory_space=pl.ANY), pl.BlockSpec(memory_space=pltpu.SMEM)
    V, D = pltpu.VMEM, pltpu.SemaphoreType.DMA
    scratch = [
        V((F, owned), F32), V((nblk, 1, TB), jnp.int32), V((H, H), F32), V((H, H), F32),
        V((1, H), F32), V((cols, H), F32),
        V((nn, CAP, TB, TB), F32),
        V((nblk, 2 * F, TB), BF),
        V((NCH, nx, slots, FC, TB), F32), V((NCH, nx, slots, FC, TB), F32),
        V((3, NCH, nblk, FC, TB), F32), V((NCH, 2, nblk, FC, TB), F32),
        V((H, cols), F32),
        V((NCH, nf, FC, cols), F32), V((NCH, nf, FC, cols), F32),
        V((H, H), BF), V((H, H), BF), V((H, H), BF), V((H, H), BF),
        V((NCH, H // NCH, H), BF), V((NCH, H // NCH, H), BF),
        V((NCH, H, H // NCH), BF), V((NCH, H, H // NCH), BF),
        V((H, cols), F32), V((H, cols), F32),
        V((H, cols), BF), V((H, cols), BF),
        V((cols, H), F32),
        V((NCH, nf, Q, FC, TB), F32),
        [V((nblk, FC, TB), F32) for _ in range(NCH)],
        [[V((nblk, FC, TB), F32) for _ in range(2)] for _ in range(NCH)],
        V((nf, Q, F, TB), F32), V((nblk, F, TB), F32),
        V((NCH, nx, slots, FC, TB), F32), V((NCH, nx, slots, FC, TB), F32),
        V((nblk, F, TB), F32), V((F, owned), F32),
        V((nf, 2 * F + 8, H), F32), V((nf, 2 * F + 8, H), F32),
        V((nx, RX + 8, H), F32), V((nx, RX + 8, H), F32),
        V((RX + 8, H), F32), V((nz, RX + 8, H), F32),
        V((RX, H), F32), V((nx, RX, H), F32),
        V((2, nf * nx // 2, RX, H), F32), V((1, H), F32),
        pltpu.SMEM((2, CAP, nn), jnp.int32),
        D((6,)), D((nn,)),
        D((nf,)), D((nf,)),
        D((2,)), D((2,)),
        D((NCH, nx, 7)), D((NCH, nx, 7)),
        D((NCH, 2)), D((NCH, 2)),
        D((NCH, nf)), D((NCH, nf)),
        D((NCH, nf)), D((NCH, nf)),
        D((NCH, 2)), D((NCH, 2)),
        D((nf,)), D((nf,)),
        D((NCH, nx, 7)), D((NCH, nx, 7)),
        D((nf,)), D((nf,)),
        D((nx,)), D((nx,)),
        D((nz,)), D((nz,)),
        D((nx,)), D((nx,)),
        D((2, nf)), D((2, nf)),
        D((5,)),
    ]
    act, gf, gs, gn, gb = pl.pallas_call(
        functools.partial(kernel, nn, nf, nx),
        out_shape=[
            jax.ShapeDtypeStruct((cols, H), F32),
            jax.ShapeDtypeStruct((F, owned), F32),
            jax.ShapeDtypeStruct((nf * nx // 2, RX, H), F32),
            jax.ShapeDtypeStruct((nf * nx // 2, RX, H), F32),
            jax.ShapeDtypeStruct((1, H), F32),
        ],
        in_specs=[anyw, anyw, smem, smem, anyw, anyw, anyw, anyw, anyw],
        out_specs=[anyw] * 5,
        scratch_shapes=scratch,
        compiler_params=pltpu.CompilerParams(
            collective_id=0, has_side_effects=True, vmem_limit_bytes=62 * 1024 * 1024
        ),
    )(
        node_feats, tiles, send_col.T, recv_row.T, degree.reshape(nblk, 1, TB),
        w_self, w_neigh, bias.reshape(1, H), cotangent,
    )
    results = [act, gf, gs.reshape(H, H), gn.reshape(H, H), gb]
    act, gf, gs, gn, gb = pl.pallas_call(
        hand_over,
        out_shape=[jax.ShapeDtypeStruct(r.shape, r.dtype) for r in results],
        in_specs=[anyw] * 5,
        out_specs=[anyw] * 5,
        scratch_shapes=[V(r.shape, r.dtype) for r in results] + [D((2, 5))],
        compiler_params=pltpu.CompilerParams(vmem_limit_bytes=62 * 1024 * 1024),
    )(*results)
    return act, gf, gs, gn, gb.reshape(H)


def solution(mesh):
    return jax.shard_map(
        functools.partial(shards, mesh.shape["node"], mesh.shape["feat"], NX),
        mesh=mesh,
        in_specs=(
            P("feat", "node"),
            P("node", None, None, None),
            P("node", None),
            P("node", None),
            P("node"),
            P(),
            P(),
            P(),
            P(("node", "feat"), None),
        ),
        out_specs=(P(("node", "feat"), None), P("feat", "node"), P(), P(), P()),
        check_vma=False,
    )
```

```python
import functools

import jax
import jax.numpy as jnp
from jax import lax
from jax.experimental import pallas as pl
from jax.experimental.pallas import tpu as pltpu
from jax.sharding import PartitionSpec as P

TB = 128
CAP = 4
NX = 4
NCH = 2
BF = jnp.bfloat16
F32 = jnp.float32
NN_DIMS = (((1,), (0,)), ((), ()))
NT_DIMS = (((1,), (1,)), ((), ()))
MESH = pl.DeviceIdType.MESH


def shift(t):
    return (2 * (t % 2) - 1) * ((t + 1) // 2)


def split(x):
    hi = x.astype(BF)
    return hi, (x - hi.astype(F32)).astype(BF)


def dot(a, b, dims):
    return lax.dot_general(a, b, dims, preferred_element_type=F32)


def dot3(a, b, dims):
    return dot(a[0], b[0], dims) + dot(a[0], b[1], dims) + dot(a[1], b[0], dims)


def total(ref, n):
    return sum((ref[i] for i in range(1, n)), ref[0])


def kernel(
    nn, nf, nx,
    feats_a, tiles, scol, rrow, deg_a, wself_a, wneigh_a, bias_a, cot_a,
    act_o, gf_o, gs_o, gn_o, gb_o,
    feats, deg, wself, wneigh, bias, cot,
    tv, tb, fs, sb, rb, acc, dr, xall, nsd, nall, wsh, wsl, wsth, wstl, wnh, wnl, wnth, wntl,
    cott, pret, gh, gl, act_v, gsd, grc, gnb, ssd, srv, bsd, brv, acc2, gf_v,
    r1s, r1r, r2s, r2r, r3s, r3r, r4s, r4r, outw, gb_v, rtab,
    isem, tsem, xss, xrs, mss, mrs, fss, frs, frn, dss, drs, nss, nrs, gss, grs, ess, ers, sss, srs, bss, brs, brn,
    r1ss, r1rs, r2ss, r2rs, r3ss, r3rs, r4ss, r4rs, r5ss, r5rs, osem,
):
    nz = nn // nx
    F = feats.shape[0]
    nblk = feats.shape[1] // TB
    Q = nblk // nf
    H = wself.shape[0]
    FC = F // NCH
    RX = 2 * F // nx
    W = FC // 8
    mf, mn = lax.axis_index("feat"), lax.axis_index("node")
    mx, mz = mn // nz, mn % nz

    def xat(dx):
        return (mx + dx + nx) % nx

    def zat(dz):
        return (mz + dz + nz) % nz

    def remote(src, dst, ss, rs, **where):
        return pltpu.make_async_remote_copy(
            src_ref=src, dst_ref=dst, send_sem=ss, recv_sem=rs, device_id=where, device_id_type=MESH)

    loads = [
        pltpu.make_async_copy(src, dst, isem.at[i])
        for i, (src, dst) in enumerate([
            (feats_a, feats), (wself_a, wself), (wneigh_a, wneigh), (cot_a, cot), (deg_a, deg), (bias_a, bias)])
    ]
    loads[0].start()
    def drain(ref, sem):
        pltpu.make_async_copy(ref, ref, sem).wait()

    barrier = pltpu.get_barrier_semaphore()

    @pl.loop(1, 7 * nx)
    def _(j):
        node = xat(j // 7) * nz + zat((j % 7 + 3) % 7 - 3)
        pl.semaphore_signal(barrier, inc=1, device_id={"node": node}, device_id_type=MESH)

    pl.semaphore_signal(barrier, inc=1, device_id={"node": mx * nz + zat(4)}, device_id_type=MESH)

    @pl.loop(1, nf)
    def _(k):
        pl.semaphore_signal(barrier, inc=1, device_id={"feat": (mf + k) % nf}, device_id_type=MESH)

    def owner(x, g):
        return x * nz + zat(shift(g))

    def tile_load(x, g, sem):
        d = owner(x, g)
        pltpu.make_async_copy(tiles.at[d], tv.at[d], sem).start()

    def pair(j):
        return [2 * (j % (nx // 2)) + i for i in range(2)]

    def turn(j):
        return pair(j), ((j // (nx // 2)) + 2) % 4 + 1

    for g in range(3):
        tile_load(mx, g, tsem.at[0])

    @pl.loop(0, nx // 2)
    def _(j):
        for k in pair(j):
            tile_load(xat(k + 1), 7, tsem.at[1 + j])

    @pl.loop(0, 2 * nx)
    def _(j):
        ks, t = turn(j)
        for k in ks:
            tile_load(xat(k + 1), t + 2, tsem.at[1 + nx // 2 + j])

    @pl.loop(0, nx - 1)
    def _(k):
        for g in range(3):
            tile_load(xat(k + 1), g, tsem.at[1 + nx // 2 + 2 * nx + k])

    for copy in loads[1:]:
        copy.start()
    loads[0].wait()
    for b in range(nblk):
        hi, lo = split(feats[:, b * TB:(b + 1) * TB])
        fs[b, :F, :TB] = hi
        fs[b, :F, TB:] = hi
        fs[b, F:, :TB] = lo
        fs[b, F:, TB:] = jnp.zeros_like(lo)
    acc[...] = jnp.zeros_like(acc)
    acc2[...] = jnp.zeros_like(acc2)

    def tile_forward(x, g):
        d = owner(x, g)
        for c in range(CAP):
            halves = jnp.concatenate(split(tv[d, c]), axis=1)
            tb[d, c] = halves
            o = dot(fs[scol[c, d]], halves, NT_DIMS)
            res = o[:F] + o[F:]
            for h in range(NCH):
                sb[h, x, 4 * g + c] = res[h * FC:(h + 1) * FC]

    drain(tv.at[pl.ds(0, 3)], tsem.at[0])
    for g in range(3):
        tile_forward(mx, g)
    pl.semaphore_wait(barrier, 7 * nx - 1 + 1 + nf - 1)

    def m_copy(i):
        return remote(rrow, rtab.at[i], mss, mrs, node=mx * nz + zat(2 * i - 1))

    for i in range(2):
        m_copy(i).start()

    def x_copy(to):
        cols = pl.ds(pl.multiple_of(to * (Q * TB), Q * TB), Q * TB)
        rows = pl.ds(pl.multiple_of(mf * F, F), F)
        return remote(feats.at[:, cols], xall.at[rows, :], xss, xrs, feat=to)

    @pl.loop(1, nf)
    def _(k):
        x_copy((mf + k) % nf).start()

    own_rows = pl.ds(pl.multiple_of(mf * F, F), F)
    xall[own_rows, :] = feats[:, pl.ds(pl.multiple_of(mf * (Q * TB), Q * TB), Q * TB)]

    def place(t):
        if not isinstance(t, int):
            return pl.ds(4 * t + 8, 4)
        return pl.ds(0, 12) if t == 0 else pl.ds(4 * t + 8, 4) if t < 5 else pl.ds(18 + 2 * t, 2)

    def arrival(per_pair, single, h, k, t):
        return single.at[h, k] if isinstance(t, int) and t == 0 else per_pair.at[h, k // 2, t - 1]

    def f_copy(h, k, t):
        x, at = xat(k + 1), place(t)
        return remote(sb.at[h, x, at], rb.at[h, mx, at], fss.at[k // (nx - 1)], arrival(frs, frn, h, k, t),
                      node=x * nz + zat(shift(t)))

    def b_copy(h, k, t):
        x, at = xat(k + 1), place(t)
        return remote(bsd.at[h, x, at], brv.at[h, mx, at], bss.at[k // (nx - 1)], arrival(brs, brn, h, k, t),
                      node=x * nz + zat(-shift(t)))

    def f_arrived(h, k, t):
        count = 1 if isinstance(t, int) and t == 0 else 2
        drain(rb.at[h, pl.ds(0, count), place(t)], arrival(frs, frn, h, k, t))

    def b_arrived(h, k, t):
        count = 1 if isinstance(t, int) and t == 0 else 2
        drain(brv.at[h, pl.ds(0, count), place(t)], arrival(brs, brn, h, k, t))

    @pl.loop(0, nx // 2)
    def _(j):
        drain(tv.at[pl.ds(0, 2)], tsem.at[1 + j])
        for k in pair(j):
            tile_forward(xat(k + 1), 7)
            f_copy(0, k, 5).start()
            f_copy(0, k, 6).start()

    @pl.loop(0, 2 * nx)
    def _(j):
        ks, t = turn(j)
        drain(tv.at[pl.ds(0, 2)], tsem.at[1 + nx // 2 + j])
        for k in ks:
            tile_forward(xat(k + 1), t + 2)
            f_copy(0, k, t).start()

    @pl.loop(0, nx - 1)
    def _(k):
        drain(tv.at[pl.ds(0, 3)], tsem.at[1 + nx // 2 + 2 * nx + k])
        for g in range(3):
            tile_forward(xat(k + 1), g)
        f_copy(0, k, 0).start()

    for h in range(1, NCH):
        @pl.loop(0, nx)
        def _(k):
            f_copy(h, k, 5).start()
            f_copy(h, k, 6).start()

        @pl.loop(0, 2 * nx)
        def _(j):
            ks, t = turn(j)
            for k in ks:
                f_copy(h, k, t).start()

        @pl.loop(0, nx - 1)
        def _(k):
            f_copy(h, k, 0).start()

    for copy in loads[1:]:
        copy.wait()
    ws = wself[...]
    wsh[...], wsl[...] = split(ws)
    wsth[...], wstl[...] = split(ws.T)
    for h in range(NCH):
        rows = jnp.concatenate(
            [wneigh[f * F + h * FC:f * F + (h + 1) * FC, :] for f in range(nf)], axis=0)
        wnh[h], wnl[h] = split(rows)
        wnth[h], wntl[h] = split(rows.T)
    for q in range(Q):
        cott[:, q * TB:(q + 1) * TB] = cot[q * TB:(q + 1) * TB, :].T
    bias_t = jnp.broadcast_to(bias[...], (TB, H)).T

    if nf > 1:
        drain(xall.at[pl.ds(0, (nf - 1) * F)], xrs)
    for q in range(Q):
        cols = slice(q * TB, (q + 1) * TB)
        pret[:, cols] = bias_t + dot3((wsth[...], wstl[...]), split(xall[:, cols]), NN_DIMS)
    drain(rtab, mrs)

    def add(to, vals, dest):
        tiles_of = [v.reshape(-1, 8, TB) for v in vals]
        wanted = [jnp.full((8, TB), r, jnp.int32) for r in dest]

        @pl.loop(0, nblk // 8)
        def _(k):
            near = [w - k * 8 for w in wanted]
            sums = [to[k * 8 + i].reshape(-1, 8, TB) for i in range(8)]
            for i in range(8):
                parts = [jnp.where((r == i)[None], v, 0.0) for v, r in zip(tiles_of, near)]
                while len(parts) > 1:
                    parts = [a + b for a, b in zip(parts[::2], parts[1::2])] + parts[len(parts) // 2 * 2:]
                sums[i] = sums[i] + parts[0]
            for i in range(8):
                to[k * 8 + i] = sums[i].reshape(to.shape[1:])

    def add_plane(h, x, ref):
        s = x * nz + mz
        for g in range(3):
            rows = [rrow[c, s] if g == 0 else rtab[g - 1, c, s] for c in range(CAP)]
            add(acc.at[g, h], [ref[h, x, 4 * g + c] for c in range(CAP)], rows)

    def d_copy(h, w, i):
        return remote(acc.at[1 + i, h, :, w], dr.at[h, i, :, w], dss, drs.at[h, w], node=mx * nz + zat(1 - 2 * i))

    for h in range(NCH):
        add_plane(h, mx, sb)

        @pl.loop(0, nx // 2)
        def _(j):
            for i in range(2):
                vals, dest = [], []
                f_arrived(h, 2 * j, 5 + i)
                for k in pair(j):
                    x = xat(-1 - k)
                    s = x * nz + zat(-shift(5 + i))
                    vals += [rb[h, x, 28 + 2 * i + c] for c in range(2)]
                    dest += [rtab[i, 2 * i + c, s] for c in range(2)]
                add(acc.at[1 + i, h], vals, dest)

        @pl.loop(0, 2 * nx)
        def _(j):
            ks, t = turn(j)
            side = 1 - t % 2
            vals, dest = [], []
            f_arrived(h, ks[0], t)
            for k in ks:
                x = xat(-1 - k)
                s = x * nz + zat(-shift(t))
                vals += [rb[h, x, 4 * t + 8 + c] for c in range(CAP)]
                dest += [rtab[side, c, s] for c in range(CAP)]
            add(acc.at[1 + side, h], vals, dest)

        @pl.loop(0, nx - 1)
        def _(k):
            f_arrived(h, k, 0)
            add_plane(h, xat(-1 - k), rb)

        for w in range(W):
            for i in range(2):
                d_copy(h, w, i).start()

    def n_copy(h, w, to):
        rows = pl.ds(8 * w, 8)
        return remote(nsd.at[h, to, rows], nall.at[h, mf, rows], nss, nrs.at[h, w], feat=to)

    for h in range(NCH):
        for w in range(W):
            drain(dr.at[h, :, :, w], drs.at[h, w])

            @pl.loop(0, nf)
            def _(f):
                for q in range(Q):
                    b = f * Q + q
                    nsd[h, f, w * 8:(w + 1) * 8, q * TB:(q + 1) * TB] = acc[0, h, b, w] + dr[h, 0, b, w] + dr[h, 1, b, w]

            @pl.loop(1, nf)
            def _(k):
                n_copy(h, w, (mf + k) % nf).start()

        nall[h, mf] = nsd[h, mf]

    inv = [1.0 / deg[mf * Q + q].astype(F32) for q in range(Q)]
    for h in range(NCH):
        for w in range(W if nf > 1 else 0):
            drain(nall.at[h, pl.ds(0, nf - 1), pl.ds(8 * w, 8)], nrs.at[h, w])

        for q in range(Q):
            cols = slice(q * TB, (q + 1) * TB)
            nb = nall[h, :, :, cols].reshape(nf * FC, TB) * inv[q]
            nall[h, :, :, cols] = nb.reshape(nf, FC, TB)
            pre = pret[:, cols] + dot3((wnth[h], wntl[h]), split(nb), NN_DIMS)
            if h < NCH - 1:
                pret[:, cols] = pre
            else:
                sig = 1.0 / (1.0 + jnp.exp(-pre))
                pret[:, cols] = pre * sig
                g = cott[:, cols] * (sig * (1.0 + pre * (1.0 - sig)))
                gh[:, cols], gl[:, cols] = split(g)
    def g_copy(h, w, to):
        blocks, rows = pl.ds(pl.multiple_of(mf * Q, Q), Q), pl.ds(8 * w, 8)
        return remote(gsd.at[h, to, :, rows], grc[h].at[blocks, rows], gss, grs.at[h, w], feat=to)

    for h in range(NCH):
        for q in range(Q):
            cols = slice(q * TB, (q + 1) * TB)
            back = dot3((wnh[h], wnl[h]), (gh[:, cols], gl[:, cols]), NN_DIMS) * inv[q]
            for f in range(nf):
                gsd[h, f, q] = back[f * FC:(f + 1) * FC]

        for w in range(W):
            @pl.loop(1, nf)
            def _(k):
                g_copy(h, w, (mf + k) % nf).start()

        for q in range(Q):
            grc[h][mf * Q + q] = gsd[h, mf, q]

    def r1_copy(to):
        return remote(r1s.at[to], r1r.at[mf], r1ss, r1rs, feat=to)

    part_self = dot3(split(xall[...]), (gh[...], gl[...]), NT_DIMS)
    for f in range(nf):
        r1s[f, :F] = part_self[f * F:(f + 1) * F]
    for h in range(NCH):
        part = dot3(split(nall[h].reshape(nf * FC, Q * TB)), (gh[...], gl[...]), NT_DIMS)
        for f in range(nf):
            r1s[f, F + h * FC:F + (h + 1) * FC] = part[f * FC:(f + 1) * FC]
    ones = jnp.ones((16, Q * TB), BF)
    part_bias = (dot(ones, gh[...], NT_DIMS) + dot(ones, gl[...], NT_DIMS))[:8]
    for f in range(nf):
        r1s[f, 2 * F:] = part_bias

    @pl.loop(1, nf)
    def _(k):
        r1_copy((mf + k) % nf).start()

    r1r[mf] = r1s[mf]

    def e_copy(h, w, i):
        rows = pl.ds(8 * w, 8)
        return remote(grc[h].at[:, rows], gnb[h][i].at[:, rows], ess, ers.at[h], node=mx * nz + zat(2 * i - 1))

    for h in range(NCH):
        for w in range(W):
            if nf > 1:
                drain(grc[h].at[pl.ds(0, (nf - 1) * Q), pl.ds(8 * w, 8)], grs.at[h, w])
            for i in range(2):
                e_copy(h, w, i).start()

    for q in range(Q):
        cols = slice(q * TB, (q + 1) * TB)
        act_v[cols, :] = pret[:, cols].T
    act_copy = pltpu.make_async_copy(act_v, act_o, osem.at[0])
    act_copy.start()

    def s_copy(to):
        blocks = pl.ds(pl.multiple_of(mf * Q, Q), Q)
        return remote(ssd.at[to], srv.at[blocks], sss, srs, feat=to)

    for q in range(Q):
        cols = slice(q * TB, (q + 1) * TB)
        back = dot3((wsh[...], wsl[...]), (gh[:, cols], gl[:, cols]), NN_DIMS)
        for f in range(nf):
            ssd[f, q] = back[f * F:(f + 1) * F]

    @pl.loop(1, nf)
    def _(k):
        s_copy((mf + k) % nf).start()

    for q in range(Q):
        srv[mf * Q + q] = ssd[mf, q]

    def pick(src, r):
        return src[jnp.maximum(r, 0)] * jnp.where(r >= 0, 1.0, 0.0)

    def pick_plane(h, x, ref):
        s = x * nz + mz
        for g in range(3):
            src = grc[h] if g == 0 else gnb[h][g - 1]
            for c in range(CAP):
                ref[h, x, 4 * g + c] = pick(src, rrow[c, s] if g == 0 else rtab[g - 1, c, s])

    def pick_all(h):
        drain(acc.at[pl.ds(0, 2), h], ers.at[h])

        @pl.loop(0, nx)
        def _(j):
            x = xat(j + 1)
            for i in range(2):
                s = x * nz + zat(-shift(5 + i))
                for c in range(2):
                    bsd[h, x, 28 + 2 * i + c] = pick(gnb[h][i], rtab[i, 2 * i + c, s])
                b_copy(h, j, 5 + i).start()

        for t in (3, 4, 1, 2):
            @pl.loop(0, nx)
            def _(j):
                x = xat(j + 1)
                s = x * nz + zat(-shift(t))
                side = 1 - t % 2
                for c in range(CAP):
                    bsd[h, x, 4 * t + 8 + c] = pick(gnb[h][side], rtab[side, c, s])
                b_copy(h, j, t).start()

        @pl.loop(0, nx - 1)
        def _(j):
            x = xat(j + 1)
            pick_plane(h, x, bsd)
            b_copy(h, j, 0).start()

        pick_plane(h, mx, brv)

    HALF = NCH // 2

    if nf > 1:
        drain(r1r.at[pl.ds(0, nf - 1)], r1rs)
    bias_sum = sum((r1r[f, 2 * F:] for f in range(1, nf)), r1r[0, 2 * F:])
    for x in range(nx):
        rows = slice(x * RX, (x + 1) * RX)
        r2s[x, :RX] = sum((r1r[f, rows] for f in range(1, nf)), r1r[0, rows])
        r2s[x, RX:] = bias_sum

    def r2_copy(x):
        return remote(r2s.at[x], r2r.at[mx], r2ss, r2rs, node=x * nz + mz)

    @pl.loop(1, nx)
    def _(k):
        r2_copy(xat(k)).start()

    r2r[mx] = r2s[mx]
    for h in range(HALF):
        pick_all(h)

    drain(r2r.at[pl.ds(0, nx - 1)], r2rs)
    r3s[...] = total(r2r, nx)

    def r3_copy(z):
        return remote(r3s, r3r.at[mz], r3ss, r3rs, node=mx * nz + z)

    @pl.loop(1, nz)
    def _(k):
        r3_copy(zat(k)).start()

    r3r[mz] = r3s[...]
    for h in range(HALF, NCH):
        pick_all(h)

    others = (nf - 1) * nx // 2
    if nf > 1:
        drain(xall.at[pl.ds(0, (nf - 1) * F)], xss)
        drain(r1s.at[pl.ds(0, nf - 1)], r1ss)
        drain(nsd.at[:, pl.ds(0, nf - 1)], nss)
        drain(gsd.at[:, pl.ds(0, nf - 1)], gss)
    drain(sb.at[:, pl.ds(0, nx - 1)], fss.at[0])
    drain(sb.at[:, 0, pl.ds(0, 20)], fss.at[1])
    drain(acc.at[pl.ds(0, 2)], dss)
    drain(acc.at[pl.ds(0, 2)], ess)
    drain(rtab, mss)
    drain(r2r.at[pl.ds(0, nx - 1)], r2ss)

    def tile_backward(p, groups):
        outs, dest = [], []
        for x, g in groups:
            d = owner(x, g)
            for c in range(CAP):
                a = jnp.concatenate([brv[h, x, 4 * g + c] for h in range(p * HALF, (p + 1) * HALF)], axis=0)
                o = dot(jnp.concatenate(split(a), axis=0), tb[d, c], NN_DIMS)
                outs.append(o[:F // 2, :TB] + o[F // 2:, :TB] + o[:F // 2, TB:])
                dest.append(scol[c, d])
        add(acc2.at[p], outs, dest)

    def arrived(p, k, t):
        for h in range(p * HALF, (p + 1) * HALF):
            b_arrived(h, k, t)

    def near(p):
        @pl.loop(0, nx - 1)
        def _(k):
            arrived(p, k, 0)
            tile_backward(p, [(xat(-1 - k), g) for g in range(3)])

    def far(p):
        @pl.loop(0, nx // 2)
        def _(j):
            arrived(p, 2 * j, 5)
            arrived(p, 2 * j, 6)
            tile_backward(p, [(xat(-1 - k), 7) for k in pair(j)])

    def middle(p, start, stop):
        @pl.loop(start, stop)
        def _(j):
            ks, t = turn(j)
            arrived(p, ks[0], t)
            tile_backward(p, [(xat(-1 - k), t + 2) for k in ks])

    for p in range(2):
        tile_backward(p, [(mx, g) for g in range(3)])
    near(0)
    far(0)
    middle(0, 0, 2 * nx)

    drain(r3r.at[pl.ds(0, nz - 1)], r3rs)
    grads = total(r3r, nz)
    r4s[...] = grads[:RX]
    gb_v[...] = grads[RX:RX + 1]

    def r4_copy(x):
        return remote(r4s, r4r.at[mx], r4ss, r4rs, node=x * nz + mz)

    @pl.loop(1, nx)
    def _(k):
        r4_copy(xat(k)).start()

    r4r[mx] = r4s[...]

    drain(r3r.at[pl.ds(0, nz - 1)], r3ss)
    if nf > 1:
        drain(ssd.at[pl.ds(0, nf - 1)], sss)

    def r5_copy(i, to):
        part = r4r.at[pl.ds(i * (nx // 2), nx // 2)]
        rows = pl.ds(pl.multiple_of(mf * (nx // 2), nx // 2), nx // 2)
        return remote(part, outw.at[i, rows], r5ss, r5rs, feat=to)

    near(1)

    drain(r4r.at[pl.ds(0, nx - 1)], r4rs)
    for i in range(2):
        @pl.loop(1, nf)
        def _(k):
            r5_copy(i, (mf + k) % nf).start()

        for x in range(nx // 2):
            outw[i, mf * (nx // 2) + x] = r4r[i * (nx // 2) + x]
    far(1)
    middle(1, 0, 2 * nx)

    if nf > 1:
        drain(srv.at[pl.ds(0, (nf - 1) * Q)], srs)
    for b in range(nblk):
        gf_v[:, b * TB:(b + 1) * TB] = srv[b] + jnp.concatenate([acc2[0, b], acc2[1, b]], axis=0)
    gf_copy = pltpu.make_async_copy(gf_v, gf_o, osem.at[1])
    gf_copy.start()
    if nf > 1:
        drain(outw.at[:, pl.ds(0, others)], r5rs)
    tail = [
        pltpu.make_async_copy(outw.at[0], gs_o, osem.at[2]),
        pltpu.make_async_copy(outw.at[1], gn_o, osem.at[3]),
        pltpu.make_async_copy(gb_v, gb_o, osem.at[4]),
    ]
    for copy in tail:
        copy.start()

    if nf > 1:
        drain(outw.at[:, pl.ds(0, others)], r5ss)
    drain(r4r.at[pl.ds(0, nx - 1)], r4ss)
    drain(bsd.at[:, pl.ds(0, nx - 1)], bss.at[0])
    drain(bsd.at[:, 0, pl.ds(0, 20)], bss.at[1])
    act_copy.wait()
    gf_copy.wait()
    for copy in tail:
        copy.wait()


def hand_over(*refs):
    n = (len(refs) - 1) // 3
    sem = refs[-1]
    takes = [pltpu.make_async_copy(refs[i], refs[2 * n + i], sem.at[0, i]) for i in range(n)]
    gives = [pltpu.make_async_copy(refs[2 * n + i], refs[n + i], sem.at[1, i]) for i in range(n)]
    for take in takes:
        take.start()
    for take, give in zip(takes, gives):
        take.wait()
        give.start()
    for give in gives:
        give.wait()


def shards(nn, nf, nx, node_feats, tiles, send_col, recv_row, degree, w_self, w_neigh, bias, cotangent):
    F, owned = node_feats.shape
    nz = nn // nx
    nblk = owned // TB
    Q = nblk // nf
    H = w_self.shape[0]
    FC = F // NCH
    RX = 2 * F // nx
    cols = Q * TB
    slots = nz * CAP
    anyw, smem = pl.BlockSpec(memory_space=pl.ANY), pl.BlockSpec(memory_space=pltpu.SMEM)
    V, D = pltpu.VMEM, pltpu.SemaphoreType.DMA
    scratch = [
        V((F, owned), F32), V((nblk, 1, TB), jnp.int32), V((H, H), F32), V((H, H), F32),
        V((1, H), F32), V((cols, H), F32),
        V((nn, CAP, TB, TB), F32), V((nn, CAP, TB, 2 * TB), BF),
        V((nblk, 2 * F, 2 * TB), BF),
        V((NCH, nx, slots, FC, TB), F32), V((NCH, nx, slots, FC, TB), F32),
        V((3, NCH, nblk, FC // 8, 8, TB), F32), V((NCH, 2, nblk, FC // 8, 8, TB), F32),
        V((H, cols), F32),
        V((NCH, nf, FC, cols), F32), V((NCH, nf, FC, cols), F32),
        V((H, H), BF), V((H, H), BF), V((H, H), BF), V((H, H), BF),
        V((NCH, H // NCH, H), BF), V((NCH, H // NCH, H), BF),
        V((NCH, H, H // NCH), BF), V((NCH, H, H // NCH), BF),
        V((H, cols), F32), V((H, cols), F32),
        V((H, cols), BF), V((H, cols), BF),
        V((cols, H), F32),
        V((NCH, nf, Q, FC, TB), F32),
        [V((nblk, FC, TB), F32) for _ in range(NCH)],
        [[V((nblk, FC, TB), F32) for _ in range(2)] for _ in range(NCH)],
        V((nf, Q, F, TB), F32), V((nblk, F, TB), F32),
        V((NCH, nx, slots, FC, TB), F32), V((NCH, nx, slots, FC, TB), F32),
        V((2, nblk, F // 2, TB), F32), V((F, owned), F32),
        V((nf, 2 * F + 8, H), F32), V((nf, 2 * F + 8, H), F32),
        V((nx, RX + 8, H), F32), V((nx, RX + 8, H), F32),
        V((RX + 8, H), F32), V((nz, RX + 8, H), F32),
        V((RX, H), F32), V((nx, RX, H), F32),
        V((2, nf * nx // 2, RX, H), F32), V((1, H), F32),
        pltpu.SMEM((2, CAP, nn), jnp.int32),
        D((6,)), D((3 * nx + nx // 2,)),
        D, D, D, D,
        D((2,)), D((NCH, nx // 2, 6)), D((NCH, nx - 1)),
        D, D((NCH, FC // 8)), D, D((NCH, FC // 8)), D, D((NCH, FC // 8)),
        D, D((NCH,)), D, D,
        D((2,)), D((NCH, nx // 2, 6)), D((NCH, nx - 1)),
        *[D] * 10,
        D((5,)),
    ]
    act, gf, gs, gn, gb = pl.pallas_call(
        functools.partial(kernel, nn, nf, nx),
        out_shape=[
            jax.ShapeDtypeStruct((cols, H), F32),
            jax.ShapeDtypeStruct((F, owned), F32),
            jax.ShapeDtypeStruct((nf * nx // 2, RX, H), F32),
            jax.ShapeDtypeStruct((nf * nx // 2, RX, H), F32),
            jax.ShapeDtypeStruct((1, H), F32),
        ],
        in_specs=[anyw, anyw, smem, smem, anyw, anyw, anyw, anyw, anyw],
        out_specs=[anyw] * 5,
        scratch_shapes=scratch,
        compiler_params=pltpu.CompilerParams(
            collective_id=0, has_side_effects=True, vmem_limit_bytes=62 * 1024 * 1024
        ),
    )(
        node_feats, tiles, send_col.T, recv_row.T, degree.reshape(nblk, 1, TB),
        w_self, w_neigh, bias.reshape(1, H), cotangent,
    )
    results = [act, gf, gs.reshape(H, H), gn.reshape(H, H), gb]
    act, gf, gs, gn, gb = pl.pallas_call(
        hand_over,
        out_shape=[jax.ShapeDtypeStruct(r.shape, r.dtype) for r in results],
        in_specs=[anyw] * 5,
        out_specs=[anyw] * 5,
        scratch_shapes=[V(r.shape, r.dtype) for r in results] + [D((2, 5))],
        compiler_params=pltpu.CompilerParams(vmem_limit_bytes=62 * 1024 * 1024),
    )(*results)
    return act, gf, gs, gn, gb.reshape(H)


def solution(mesh):
    return jax.shard_map(
        functools.partial(shards, mesh.shape["node"], mesh.shape["feat"], NX),
        mesh=mesh,
        in_specs=(
            P("feat", "node"),
            P("node", None, None, None),
            P("node", None),
            P("node", None),
            P("node"),
            P(),
            P(),
            P(),
            P(("node", "feat"), None),
        ),
        out_specs=(P(("node", "feat"), None), P("feat", "node"), P(), P(), P()),
        check_vma=False,
    )
```

```python
import functools

import jax
import jax.numpy as jnp
from jax import lax
from jax.experimental import pallas as pl
from jax.experimental.pallas import tpu as pltpu
from jax.sharding import PartitionSpec as P

TB = 128
CAP = 4
NX = 4
NCH = 2
BF = jnp.bfloat16
F32 = jnp.float32
NN_DIMS = (((1,), (0,)), ((), ()))
NT_DIMS = (((1,), (1,)), ((), ()))
MESH = pl.DeviceIdType.MESH


def shift(t):
    return (2 * (t % 2) - 1) * ((t + 1) // 2)


def split(x):
    hi = x.astype(BF)
    return hi, (x - hi.astype(F32)).astype(BF)


def dot(a, b, dims):
    return lax.dot_general(a, b, dims, preferred_element_type=F32)


def dot3(a, b, dims):
    return dot(a[0], b[0], dims) + dot(a[0], b[1], dims) + dot(a[1], b[0], dims)


def total(ref, n):
    return sum((ref[i] for i in range(1, n)), ref[0])


def kernel(
    nn, nf, nx,
    feats_a, tiles, scol_a, rrow_a, deg_a, wself_a, wneigh_a, bias_a, cot_a,
    act_o, gf_o, gs_o, gn_o, gb_o,
    feats, scol, rrow, deg, wself, wneigh, bias, cot,
    tv, tb, fs, sb, rb, acc, dr, xall, nsd, nall, wsh, wsl, wsth, wstl, wnh, wnl, wnth, wntl,
    cott, pret, gh, gl, act_v, gsd, grc, gnb, ssd, srv, bsd, brv, acc2, gf_v,
    r1s, r1r, r2s, r2r, r3s, r3r, r4s, r4r, outw, gb_v, rtab,
    isem, tsem, xss, xrs, mss, mrs, fss, frs, frn, dss, drs, nss, nrs, gss, grs, ess, ers, sss, srs, bss, brs, brn,
    r1ss, r1rs, r2ss, r2rs, r3ss, r3rs, r4ss, r4rs, r5ss, r5rs, osem,
):
    nz = nn // nx
    F = feats.shape[0]
    nblk = feats.shape[1] // TB
    Q = nblk // nf
    H = wself.shape[0]
    FC = F // NCH
    RZ = 2 * F // nz
    W = FC // 8
    mf, mn = lax.axis_index("feat"), lax.axis_index("node")
    mx, mz = mn // nz, mn % nz

    def xat(dx):
        return (mx + dx + nx) % nx

    def zat(dz):
        return (mz + dz + nz) % nz

    def remote(src, dst, ss, rs, **where):
        return pltpu.make_async_remote_copy(
            src_ref=src, dst_ref=dst, send_sem=ss, recv_sem=rs, device_id=where, device_id_type=MESH)

    loads = [
        pltpu.make_async_copy(src, dst, isem.at[i])
        for i, (src, dst) in enumerate([
            (feats_a, feats), (scol_a, scol), (rrow_a, rrow), (wself_a, wself), (wneigh_a, wneigh), (cot_a, cot), (deg_a, deg), (bias_a, bias)])
    ]
    for copy in loads[:3]:
        copy.start()

    def drain(ref, sem):
        pltpu.make_async_copy(ref, ref, sem).wait()

    barrier = pltpu.get_barrier_semaphore()

    @pl.loop(1, 7 * nx)
    def _(j):
        node = xat(j // 7) * nz + zat((j % 7 + 3) % 7 - 3)
        pl.semaphore_signal(barrier, inc=1, device_id={"node": node}, device_id_type=MESH)

    pl.semaphore_signal(barrier, inc=1, device_id={"node": mx * nz + zat(4)}, device_id_type=MESH)

    @pl.loop(1, nf)
    def _(k):
        pl.semaphore_signal(barrier, inc=1, device_id={"feat": (mf + k) % nf}, device_id_type=MESH)

    def owner(x, g):
        return x * nz + zat(shift(g))

    def tile_load(x, g, sem):
        d = owner(x, g)
        pltpu.make_async_copy(tiles.at[d], tv.at[d], sem).start()

    def pair(j):
        return [2 * (j % (nx // 2)) + i for i in range(2)]

    def turn(j):
        return pair(j), ((j // (nx // 2)) + 2) % 4 + 1

    for g in range(3):
        tile_load(mx, g, tsem.at[0])

    @pl.loop(0, nx // 2)
    def _(j):
        for k in pair(j):
            tile_load(xat(k + 1), 7, tsem.at[1 + j])

    @pl.loop(0, 2 * nx)
    def _(j):
        ks, t = turn(j)
        for k in ks:
            tile_load(xat(k + 1), t + 2, tsem.at[1 + nx // 2 + j])

    @pl.loop(0, nx - 1)
    def _(k):
        for g in range(3):
            tile_load(xat(k + 1), g, tsem.at[1 + nx // 2 + 2 * nx + k])

    for copy in loads[3:]:
        copy.start()
    for copy in loads[:3]:
        copy.wait()
    for b in range(nblk):
        hi, lo = split(feats[:, b * TB:(b + 1) * TB])
        fs[b, :F, :TB] = hi
        fs[b, :F, TB:] = hi
        fs[b, F:, :TB] = lo
        fs[b, F:, TB:] = jnp.zeros_like(lo)
    acc[...] = jnp.zeros_like(acc)
    acc2[...] = jnp.zeros_like(acc2)

    def tile_forward(x, g):
        d = owner(x, g)
        for c in range(CAP):
            halves = jnp.concatenate(split(tv[d, c]), axis=1)
            tb[d, c] = halves
            o = dot(fs[scol[c, d]], halves, NT_DIMS)
            res = o[:F] + o[F:]
            for h in range(NCH):
                sb[h, x, 4 * g + c] = res[h * FC:(h + 1) * FC]

    drain(tv.at[pl.ds(0, 3)], tsem.at[0])
    for g in range(3):
        tile_forward(mx, g)
    pl.semaphore_wait(barrier, 7 * nx - 1 + 1 + nf - 1)

    def m_copy(i):
        return remote(rrow, rtab.at[i], mss, mrs, node=mx * nz + zat(2 * i - 1))

    for i in range(2):
        m_copy(i).start()

    def x_copy(to):
        cols = pl.ds(pl.multiple_of(to * (Q * TB), Q * TB), Q * TB)
        rows = pl.ds(pl.multiple_of(mf * F, F), F)
        return remote(feats.at[:, cols], xall.at[rows, :], xss, xrs, feat=to)

    @pl.loop(1, nf)
    def _(k):
        x_copy((mf + k) % nf).start()

    own_rows = pl.ds(pl.multiple_of(mf * F, F), F)
    xall[own_rows, :] = feats[:, pl.ds(pl.multiple_of(mf * (Q * TB), Q * TB), Q * TB)]

    def place(t):
        if not isinstance(t, int):
            return pl.ds(4 * t + 8, 4)
        return pl.ds(0, 12) if t == 0 else pl.ds(4 * t + 8, 4) if t < 5 else pl.ds(18 + 2 * t, 2)

    def arrival(per_pair, single, h, k, t):
        return single.at[h, k] if isinstance(t, int) and t == 0 else per_pair.at[h, k // 2, t - 1]

    def f_copy(h, k, t):
        x, at = xat(k + 1), place(t)
        return remote(sb.at[h, x, at], rb.at[h, mx, at], fss.at[k // (nx - 1)], arrival(frs, frn, h, k, t),
                      node=x * nz + zat(shift(t)))

    def b_copy(h, k, t):
        x, at = xat(k + 1), place(t)
        return remote(bsd.at[h, x, at], brv.at[h, mx, at], bss.at[k // (nx - 1)], arrival(brs, brn, h, k, t),
                      node=x * nz + zat(-shift(t)))

    def f_arrived(h, k, t):
        count = 1 if isinstance(t, int) and t == 0 else 2
        drain(rb.at[h, pl.ds(0, count), place(t)], arrival(frs, frn, h, k, t))

    def b_arrived(h, k, t):
        count = 1 if isinstance(t, int) and t == 0 else 2
        drain(brv.at[h, pl.ds(0, count), place(t)], arrival(brs, brn, h, k, t))

    @pl.loop(0, nx // 2)
    def _(j):
        drain(tv.at[pl.ds(0, 2)], tsem.at[1 + j])
        for k in pair(j):
            tile_forward(xat(k + 1), 7)
            f_copy(0, k, 5).start()
            f_copy(0, k, 6).start()

    @pl.loop(0, 2 * nx)
    def _(j):
        ks, t = turn(j)
        drain(tv.at[pl.ds(0, 2)], tsem.at[1 + nx // 2 + j])
        for k in ks:
            tile_forward(xat(k + 1), t + 2)
            f_copy(0, k, t).start()

    @pl.loop(0, nx - 1)
    def _(k):
        drain(tv.at[pl.ds(0, 3)], tsem.at[1 + nx // 2 + 2 * nx + k])
        for g in range(3):
            tile_forward(xat(k + 1), g)
        f_copy(0, k, 0).start()

    for h in range(1, NCH):
        @pl.loop(0, nx)
        def _(k):
            f_copy(h, k, 5).start()
            f_copy(h, k, 6).start()

        @pl.loop(0, 2 * nx)
        def _(j):
            ks, t = turn(j)
            for k in ks:
                f_copy(h, k, t).start()

        @pl.loop(0, nx - 1)
        def _(k):
            f_copy(h, k, 0).start()

    for copy in loads[3:]:
        copy.wait()
    ws = wself[...]
    wsh[...], wsl[...] = split(ws)
    wsth[...], wstl[...] = split(ws.T)
    for h in range(NCH):
        rows = jnp.concatenate(
            [wneigh[f * F + h * FC:f * F + (h + 1) * FC, :] for f in range(nf)], axis=0)
        wnh[h], wnl[h] = split(rows)
        wnth[h], wntl[h] = split(rows.T)
    for q in range(Q):
        cott[:, q * TB:(q + 1) * TB] = cot[q * TB:(q + 1) * TB, :].T
    bias_t = jnp.broadcast_to(bias[...], (TB, H)).T

    if nf > 1:
        drain(xall.at[pl.ds(0, (nf - 1) * F)], xrs)
    for q in range(Q):
        cols = slice(q * TB, (q + 1) * TB)
        pret[:, cols] = bias_t + dot3((wsth[...], wstl[...]), split(xall[:, cols]), NN_DIMS)
    drain(rtab, mrs)

    def add(to, vals, dest):
        tiles_of = [v.reshape(-1, 8, TB) for v in vals]
        wanted = [jnp.full((8, TB), r, jnp.int32) for r in dest]

        @pl.loop(0, nblk // 8)
        def _(k):
            near = [w - k * 8 for w in wanted]
            sums = [to[k * 8 + i].reshape(-1, 8, TB) for i in range(8)]
            for i in range(8):
                parts = [jnp.where((r == i)[None], v, 0.0) for v, r in zip(tiles_of, near)]
                while len(parts) > 1:
                    parts = [a + b for a, b in zip(parts[::2], parts[1::2])] + parts[len(parts) // 2 * 2:]
                sums[i] = sums[i] + parts[0]
            for i in range(8):
                to[k * 8 + i] = sums[i].reshape(to.shape[1:])

    def add_plane(h, x, ref):
        s = x * nz + mz
        for g in range(3):
            rows = [rrow[c, s] if g == 0 else rtab[g - 1, c, s] for c in range(CAP)]
            add(acc.at[g, h], [ref[h, x, 4 * g + c] for c in range(CAP)], rows)

    def d_copy(h, w, i):
        return remote(acc.at[1 + i, h, :, w], dr.at[h, i, :, w], dss, drs.at[h, w], node=mx * nz + zat(1 - 2 * i))

    for h in range(NCH):
        add_plane(h, mx, sb)

        @pl.loop(0, nx // 2)
        def _(j):
            for i in range(2):
                vals, dest = [], []
                f_arrived(h, 2 * j, 5 + i)
                for k in pair(j):
                    x = xat(-1 - k)
                    s = x * nz + zat(-shift(5 + i))
                    vals += [rb[h, x, 28 + 2 * i + c] for c in range(2)]
                    dest += [rtab[i, 2 * i + c, s] for c in range(2)]
                add(acc.at[1 + i, h], vals, dest)

        @pl.loop(0, 2 * nx)
        def _(j):
            ks, t = turn(j)
            side = 1 - t % 2
            vals, dest = [], []
            f_arrived(h, ks[0], t)
            for k in ks:
                x = xat(-1 - k)
                s = x * nz + zat(-shift(t))
                vals += [rb[h, x, 4 * t + 8 + c] for c in range(CAP)]
                dest += [rtab[side, c, s] for c in range(CAP)]
            add(acc.at[1 + side, h], vals, dest)

        @pl.loop(0, nx - 1)
        def _(k):
            f_arrived(h, k, 0)
            add_plane(h, xat(-1 - k), rb)

        for w in range(W):
            for i in range(2):
                d_copy(h, w, i).start()

    def n_copy(h, w, to):
        rows = pl.ds(8 * w, 8)
        return remote(nsd.at[h, to, rows], nall.at[h, mf, rows], nss, nrs.at[h, w], feat=to)

    for h in range(NCH):
        for w in range(W):
            drain(dr.at[h, :, :, w], drs.at[h, w])

            @pl.loop(0, nf)
            def _(f):
                for q in range(Q):
                    b = f * Q + q
                    nsd[h, f, w * 8:(w + 1) * 8, q * TB:(q + 1) * TB] = acc[0, h, b, w] + dr[h, 0, b, w] + dr[h, 1, b, w]

            @pl.loop(1, nf)
            def _(k):
                n_copy(h, w, (mf + k) % nf).start()

        nall[h, mf] = nsd[h, mf]

    inv = [1.0 / deg[mf * Q + q].astype(F32) for q in range(Q)]
    for h in range(NCH):
        for w in range(W if nf > 1 else 0):
            drain(nall.at[h, pl.ds(0, nf - 1), pl.ds(8 * w, 8)], nrs.at[h, w])

        for q in range(Q):
            cols = slice(q * TB, (q + 1) * TB)
            nb = nall[h, :, :, cols].reshape(nf * FC, TB) * inv[q]
            nall[h, :, :, cols] = nb.reshape(nf, FC, TB)
            pre = pret[:, cols] + dot3((wnth[h], wntl[h]), split(nb), NN_DIMS)
            if h < NCH - 1:
                pret[:, cols] = pre
            else:
                sig = 1.0 / (1.0 + jnp.exp(-pre))
                pret[:, cols] = pre * sig
                g = cott[:, cols] * (sig * (1.0 + pre * (1.0 - sig)))
                gh[:, cols], gl[:, cols] = split(g)
    def g_copy(h, w, to):
        blocks, rows = pl.ds(pl.multiple_of(mf * Q, Q), Q), pl.ds(8 * w, 8)
        return remote(gsd.at[h, to, :, rows], grc[h].at[blocks, rows], gss, grs.at[h, w], feat=to)

    for h in range(NCH):
        for q in range(Q):
            cols = slice(q * TB, (q + 1) * TB)
            back = dot3((wnh[h], wnl[h]), (gh[:, cols], gl[:, cols]), NN_DIMS) * inv[q]
            for f in range(nf):
                gsd[h, f, q] = back[f * FC:(f + 1) * FC]

        for w in range(W):
            @pl.loop(1, nf)
            def _(k):
                g_copy(h, w, (mf + k) % nf).start()

        for q in range(Q):
            grc[h][mf * Q + q] = gsd[h, mf, q]

    def r1_copy(to):
        return remote(r1s.at[to], r1r.at[mf], r1ss, r1rs, feat=to)

    part_self = dot3(split(xall[...]), (gh[...], gl[...]), NT_DIMS)
    for f in range(nf):
        r1s[f, :F] = part_self[f * F:(f + 1) * F]
    for h in range(NCH):
        part = dot3(split(nall[h].reshape(nf * FC, Q * TB)), (gh[...], gl[...]), NT_DIMS)
        for f in range(nf):
            r1s[f, F + h * FC:F + (h + 1) * FC] = part[f * FC:(f + 1) * FC]
    ones = jnp.ones((16, Q * TB), BF)
    part_bias = (dot(ones, gh[...], NT_DIMS) + dot(ones, gl[...], NT_DIMS))[:8]
    for f in range(nf):
        r1s[f, 2 * F:] = part_bias

    @pl.loop(1, nf)
    def _(k):
        r1_copy((mf + k) % nf).start()

    r1r[mf] = r1s[mf]

    def e_copy(h, w, i):
        rows = pl.ds(8 * w, 8)
        return remote(grc[h].at[:, rows], gnb[h][i].at[:, rows], ess, ers.at[h], node=mx * nz + zat(2 * i - 1))

    for h in range(NCH):
        for w in range(W):
            if nf > 1:
                drain(grc[h].at[pl.ds(0, (nf - 1) * Q), pl.ds(8 * w, 8)], grs.at[h, w])
            for i in range(2):
                e_copy(h, w, i).start()

    for q in range(Q):
        cols = slice(q * TB, (q + 1) * TB)
        act_v[cols, :] = pret[:, cols].T
    act_copy = pltpu.make_async_copy(act_v, act_o, osem.at[0])
    act_copy.start()

    def s_copy(to):
        blocks = pl.ds(pl.multiple_of(mf * Q, Q), Q)
        return remote(ssd.at[to], srv.at[blocks], sss, srs, feat=to)

    for q in range(Q):
        cols = slice(q * TB, (q + 1) * TB)
        back = dot3((wsh[...], wsl[...]), (gh[:, cols], gl[:, cols]), NN_DIMS)
        for f in range(nf):
            ssd[f, q] = back[f * F:(f + 1) * F]

    @pl.loop(1, nf)
    def _(k):
        s_copy((mf + k) % nf).start()

    for q in range(Q):
        srv[mf * Q + q] = ssd[mf, q]

    def pick(src, r):
        return src[jnp.maximum(r, 0)] * jnp.where(r >= 0, 1.0, 0.0)

    def pick_plane(h, x, ref):
        s = x * nz + mz
        for g in range(3):
            src = grc[h] if g == 0 else gnb[h][g - 1]
            for c in range(CAP):
                ref[h, x, 4 * g + c] = pick(src, rrow[c, s] if g == 0 else rtab[g - 1, c, s])

    def pick_far(h):
        drain(acc.at[pl.ds(0, 2), h], ers.at[h])

        @pl.loop(0, nx)
        def _(j):
            x = xat(j + 1)
            for i in range(2):
                s = x * nz + zat(-shift(5 + i))
                for c in range(2):
                    bsd[h, x, 28 + 2 * i + c] = pick(gnb[h][i], rtab[i, 2 * i + c, s])
                b_copy(h, j, 5 + i).start()

        for t in (3, 4, 1, 2):
            @pl.loop(0, nx)
            def _(j):
                x = xat(j + 1)
                s = x * nz + zat(-shift(t))
                side = 1 - t % 2
                for c in range(CAP):
                    bsd[h, x, 4 * t + 8 + c] = pick(gnb[h][side], rtab[side, c, s])
                b_copy(h, j, t).start()

    def pick_near(h):
        @pl.loop(0, nx - 1)
        def _(j):
            x = xat(j + 1)
            pick_plane(h, x, bsd)
            b_copy(h, j, 0).start()

        pick_plane(h, mx, brv)

    HALF = NCH // 2

    if nf > 1:
        drain(r1r.at[pl.ds(0, nf - 1)], r1rs)
    bias_sum = sum((r1r[f, 2 * F:] for f in range(1, nf)), r1r[0, 2 * F:])
    for z in range(nz):
        rows = slice(z * RZ, (z + 1) * RZ)
        r2s[z, :RZ] = sum((r1r[f, rows] for f in range(1, nf)), r1r[0, rows])
        r2s[z, RZ:] = bias_sum

    def r2_copy(z):
        return remote(r2s.at[z], r2r.at[mz], r2ss, r2rs, node=mx * nz + z)

    @pl.loop(1, nz)
    def _(k):
        r2_copy(zat(k)).start()

    r2r[mz] = r2s[mz]
    for h in range(HALF):
        pick_far(h)
    drain(r2r.at[pl.ds(0, nz - 1)], r2rs)
    r3s[...] = total(r2r, nz)

    def r3_copy(x):
        return remote(r3s, r3r.at[mx], r3ss, r3rs, node=x * nz + mz)

    @pl.loop(1, nx)
    def _(k):
        r3_copy(xat(k)).start()

    r3r[mx] = r3s[...]
    for h in range(HALF):
        pick_near(h)

    others = (nf - 1) * nz // 2
    if nf > 1:
        drain(xall.at[pl.ds(0, (nf - 1) * F)], xss)
        drain(r1s.at[pl.ds(0, nf - 1)], r1ss)
        drain(nsd.at[:, pl.ds(0, nf - 1)], nss)
        drain(gsd.at[:, pl.ds(0, nf - 1)], gss)
    drain(sb.at[:, pl.ds(0, nx - 1)], fss.at[0])
    drain(sb.at[:, 0, pl.ds(0, 20)], fss.at[1])
    drain(acc.at[pl.ds(0, 2)], dss)
    drain(acc.at[pl.ds(0, 2)], ess)
    drain(rtab, mss)
    drain(r2r.at[pl.ds(0, nz - 1)], r2ss)

    def tile_backward(p, groups):
        outs, dest = [], []
        for x, g in groups:
            d = owner(x, g)
            for c in range(CAP):
                a = jnp.concatenate([brv[h, x, 4 * g + c] for h in range(p * HALF, (p + 1) * HALF)], axis=0)
                o = dot(jnp.concatenate(split(a), axis=0), tb[d, c], NN_DIMS)
                outs.append(o[:F // 2, :TB] + o[F // 2:, :TB] + o[:F // 2, TB:])
                dest.append(scol[c, d])
        add(acc2.at[p], outs, dest)

    def arrived(p, k, t):
        for h in range(p * HALF, (p + 1) * HALF):
            b_arrived(h, k, t)

    def near(p):
        @pl.loop(0, nx - 1)
        def _(k):
            arrived(p, k, 0)
            tile_backward(p, [(xat(-1 - k), g) for g in range(3)])

    def far(p):
        @pl.loop(0, nx // 2)
        def _(j):
            arrived(p, 2 * j, 5)
            arrived(p, 2 * j, 6)
            tile_backward(p, [(xat(-1 - k), 7) for k in pair(j)])

    def middle(p, start, stop):
        @pl.loop(start, stop)
        def _(j):
            ks, t = turn(j)
            arrived(p, ks[0], t)
            tile_backward(p, [(xat(-1 - k), t + 2) for k in ks])

    tile_backward(0, [(mx, g) for g in range(3)])
    drain(r3r.at[pl.ds(0, nx - 1)], r3rs)
    grads = total(r3r, nx)
    r4s[...] = grads[:RZ]
    gb_v[...] = grads[RZ:RZ + 1]

    def r4_copy(z):
        return remote(r4s, r4r.at[mz], r4ss, r4rs, node=mx * nz + z)

    @pl.loop(1, nz)
    def _(k):
        r4_copy(zat(k)).start()

    r4r[mz] = r4s[...]
    for h in range(HALF, NCH):
        pick_far(h)
        pick_near(h)
    tile_backward(1, [(mx, g) for g in range(3)])
    far(0)
    middle(0, 0, 2 * nx)
    near(0)

    drain(r4r.at[pl.ds(0, nz - 1)], r4rs)
    drain(r3r.at[pl.ds(0, nx - 1)], r3ss)
    if nf > 1:
        drain(ssd.at[pl.ds(0, nf - 1)], sss)

    def r5_copy(i, to):
        part = r4r.at[pl.ds(i * (nz // 2), nz // 2)]
        rows = pl.ds(pl.multiple_of(mf * (nz // 2), nz // 2), nz // 2)
        return remote(part, outw.at[i, rows], r5ss, r5rs, feat=to)

    for i in range(2):
        @pl.loop(1, nf)
        def _(k):
            r5_copy(i, (mf + k) % nf).start()

        for z in range(nz // 2):
            outw[i, mf * (nz // 2) + z] = r4r[i * (nz // 2) + z]
    near(1)
    far(1)
    middle(1, 0, 2 * nx)

    if nf > 1:
        drain(srv.at[pl.ds(0, (nf - 1) * Q)], srs)
    for b in range(nblk):
        gf_v[:, b * TB:(b + 1) * TB] = srv[b] + jnp.concatenate([acc2[0, b], acc2[1, b]], axis=0)
    gf_copy = pltpu.make_async_copy(gf_v, gf_o, osem.at[1])
    gf_copy.start()
    if nf > 1:
        drain(outw.at[:, pl.ds(0, others)], r5rs)
    tail = [
        pltpu.make_async_copy(outw.at[0], gs_o, osem.at[2]),
        pltpu.make_async_copy(outw.at[1], gn_o, osem.at[3]),
        pltpu.make_async_copy(gb_v, gb_o, osem.at[4]),
    ]
    for copy in tail:
        copy.start()

    if nf > 1:
        drain(outw.at[:, pl.ds(0, others)], r5ss)
    drain(r4r.at[pl.ds(0, nz - 1)], r4ss)
    drain(bsd.at[:, pl.ds(0, nx - 1)], bss.at[0])
    drain(bsd.at[:, 0, pl.ds(0, 20)], bss.at[1])
    act_copy.wait()
    gf_copy.wait()
    for copy in tail:
        copy.wait()


def hand_over(*refs):
    n = (len(refs) - 1) // 3
    sem = refs[-1]
    takes = [pltpu.make_async_copy(refs[i], refs[2 * n + i], sem.at[0, i]) for i in range(n)]
    gives = [pltpu.make_async_copy(refs[2 * n + i], refs[n + i], sem.at[1, i]) for i in range(n)]
    for take in takes:
        take.start()
    for take, give in zip(takes, gives):
        take.wait()
        give.start()
    for give in gives:
        give.wait()


def shards(nn, nf, nx, node_feats, tiles, send_col, recv_row, degree, w_self, w_neigh, bias, cotangent):
    F, owned = node_feats.shape
    nz = nn // nx
    nblk = owned // TB
    Q = nblk // nf
    H = w_self.shape[0]
    FC = F // NCH
    RZ = 2 * F // nz
    cols = Q * TB
    slots = nz * CAP
    anyw = pl.BlockSpec(memory_space=pl.ANY)
    V, D = pltpu.VMEM, pltpu.SemaphoreType.DMA
    scratch = [
        V((F, owned), F32), pltpu.SMEM((CAP, nn), jnp.int32), pltpu.SMEM((CAP, nn), jnp.int32),
        V((nblk, 1, TB), jnp.int32), V((H, H), F32), V((H, H), F32),
        V((1, H), F32), V((cols, H), F32),
        V((nn, CAP, TB, TB), F32), V((nn, CAP, TB, 2 * TB), BF),
        V((nblk, 2 * F, 2 * TB), BF),
        V((NCH, nx, slots, FC, TB), F32), V((NCH, nx, slots, FC, TB), F32),
        V((3, NCH, nblk, FC // 8, 8, TB), F32), V((NCH, 2, nblk, FC // 8, 8, TB), F32),
        V((H, cols), F32),
        V((NCH, nf, FC, cols), F32), V((NCH, nf, FC, cols), F32),
        V((H, H), BF), V((H, H), BF), V((H, H), BF), V((H, H), BF),
        V((NCH, H // NCH, H), BF), V((NCH, H // NCH, H), BF),
        V((NCH, H, H // NCH), BF), V((NCH, H, H // NCH), BF),
        V((H, cols), F32), V((H, cols), F32),
        V((H, cols), BF), V((H, cols), BF),
        V((cols, H), F32),
        V((NCH, nf, Q, FC, TB), F32),
        [V((nblk, FC, TB), F32) for _ in range(NCH)],
        [[V((nblk, FC, TB), F32) for _ in range(2)] for _ in range(NCH)],
        V((nf, Q, F, TB), F32), V((nblk, F, TB), F32),
        V((NCH, nx, slots, FC, TB), F32), V((NCH, nx, slots, FC, TB), F32),
        V((2, nblk, F // 2, TB), F32), V((F, owned), F32),
        V((nf, 2 * F + 8, H), F32), V((nf, 2 * F + 8, H), F32),
        V((nz, RZ + 8, H), F32), V((nz, RZ + 8, H), F32),
        V((RZ + 8, H), F32), V((nx, RZ + 8, H), F32),
        V((RZ, H), F32), V((nz, RZ, H), F32),
        V((2, nf * nz // 2, RZ, H), F32), V((1, H), F32),
        pltpu.SMEM((2, CAP, nn), jnp.int32),
        D((8,)), D((3 * nx + nx // 2,)),
        D, D, D, D,
        D((2,)), D((NCH, nx // 2, 6)), D((NCH, nx - 1)),
        D, D((NCH, FC // 8)), D, D((NCH, FC // 8)), D, D((NCH, FC // 8)),
        D, D((NCH,)), D, D,
        D((2,)), D((NCH, nx // 2, 6)), D((NCH, nx - 1)),
        *[D] * 10,
        D((5,)),
    ]
    act, gf, gs, gn, gb = pl.pallas_call(
        functools.partial(kernel, nn, nf, nx),
        out_shape=[
            jax.ShapeDtypeStruct((cols, H), F32),
            jax.ShapeDtypeStruct((F, owned), F32),
            jax.ShapeDtypeStruct((nf * nz // 2, RZ, H), F32),
            jax.ShapeDtypeStruct((nf * nz // 2, RZ, H), F32),
            jax.ShapeDtypeStruct((1, H), F32),
        ],
        in_specs=[anyw] * 9,
        out_specs=[anyw] * 5,
        scratch_shapes=scratch,
        compiler_params=pltpu.CompilerParams(
            collective_id=0, has_side_effects=True, vmem_limit_bytes=62 * 1024 * 1024
        ),
    )(
        node_feats, tiles, send_col.T, recv_row.T, degree.reshape(nblk, 1, TB),
        w_self, w_neigh, bias.reshape(1, H), cotangent,
    )
    results = [act, gf, gs.reshape(H, H), gn.reshape(H, H), gb]
    act, gf, gs, gn, gb = pl.pallas_call(
        hand_over,
        out_shape=[jax.ShapeDtypeStruct(r.shape, r.dtype) for r in results],
        in_specs=[anyw] * 5,
        out_specs=[anyw] * 5,
        scratch_shapes=[V(r.shape, r.dtype) for r in results] + [D((2, 5))],
        compiler_params=pltpu.CompilerParams(vmem_limit_bytes=62 * 1024 * 1024),
    )(*results)
    return act, gf, gs, gn, gb.reshape(H)


def solution(mesh):
    return jax.shard_map(
        functools.partial(shards, mesh.shape["node"], mesh.shape["feat"], NX),
        mesh=mesh,
        in_specs=(
            P("feat", "node"),
            P("node", None, None, None),
            P("node", None),
            P("node", None),
            P("node"),
            P(),
            P(),
            P(),
            P(("node", "feat"), None),
        ),
        out_specs=(P(("node", "feat"), None), P("feat", "node"), P(), P(), P()),
        check_vma=False,
    )
```

```python
import functools

import jax
import jax.numpy as jnp
from jax import lax
from jax.experimental import pallas as pl
from jax.experimental.pallas import tpu as pltpu
from jax.sharding import PartitionSpec as P

TB = 128
CAP = 4
NX = 4
NCH = 2
BF = jnp.bfloat16
F32 = jnp.float32
NN_DIMS = (((1,), (0,)), ((), ()))
NT_DIMS = (((1,), (1,)), ((), ()))
MESH = pl.DeviceIdType.MESH


def shift(t):
    return (2 * (t % 2) - 1) * ((t + 1) // 2)


def split(x):
    hi = x.astype(BF)
    return hi, (x - hi.astype(F32)).astype(BF)


def dot(a, b, dims):
    return lax.dot_general(a, b, dims, preferred_element_type=F32)


def dot3(a, b, dims):
    return dot(a[0], b[0], dims) + dot(a[0], b[1], dims) + dot(a[1], b[0], dims)


def total(ref, n):
    return sum((ref[i] for i in range(1, n)), ref[0])


def kernel(
    nn, nf, nx,
    feats_a, tiles, scol_a, rrow_a, deg_a, wself_a, wneigh_a, bias_a, cot_a,
    act_o, gf_o, gs_o, gn_o, gb_o,
    feats, scol, rrow, deg, wself, wneigh, bias, cot,
    tv, tb, fs, sb, rb, acc, dr, xall, nsd, nall, wsh, wsl, wsth, wstl, wnh, wnl, wnth, wntl,
    cott, pret, gh, gl, act_v, gsd, grc, gnb, ssd, srv, bsd, brv, acc2, gf_v,
    r1s, r1r, r2s, r2r, r3s, r3r, r4s, r4r, outw, gb_v, rtab,
    isem, tsem, xss, xrs, mss, mrs, fss, frs, frn, dss, drs, nss, nrs, gss, grs, ess, ers, sss, srs, bss, brs, brn,
    r1ss, r1rs, r2ss, r2rs, r3ss, r3rs, r4ss, r4rs, r5ss, r5rs, osem,
):
    nz = nn // nx
    F = feats.shape[0]
    nblk = feats.shape[1] // TB
    Q = nblk // nf
    H = wself.shape[0]
    FC = F // NCH
    RZ = 2 * F // nz
    W = FC // 8
    mf, mn = lax.axis_index("feat"), lax.axis_index("node")
    mx, mz = mn // nz, mn % nz

    def xat(dx):
        return (mx + dx + nx) % nx

    def zat(dz):
        return (mz + dz + nz) % nz

    def remote(src, dst, ss, rs, **where):
        return pltpu.make_async_remote_copy(
            src_ref=src, dst_ref=dst, send_sem=ss, recv_sem=rs, device_id=where, device_id_type=MESH)

    loads = [
        pltpu.make_async_copy(src, dst, isem.at[i])
        for i, (src, dst) in enumerate([
            (feats_a, feats), (scol_a, scol), (rrow_a, rrow), (wself_a, wself), (wneigh_a, wneigh), (cot_a, cot), (deg_a, deg), (bias_a, bias)])
    ]
    for copy in loads[:3]:
        copy.start()

    def drain(ref, sem):
        pltpu.make_async_copy(ref, ref, sem).wait()

    barrier = pltpu.get_barrier_semaphore()

    @pl.loop(1, 7 * nx)
    def _(j):
        node = xat(j // 7) * nz + zat((j % 7 + 3) % 7 - 3)
        pl.semaphore_signal(barrier, inc=1, device_id={"node": node}, device_id_type=MESH)

    pl.semaphore_signal(barrier, inc=1, device_id={"node": mx * nz + zat(4)}, device_id_type=MESH)

    @pl.loop(1, nf)
    def _(k):
        pl.semaphore_signal(barrier, inc=1, device_id={"feat": (mf + k) % nf}, device_id_type=MESH)

    def owner(x, g):
        return x * nz + zat(shift(g))

    def tile_load(x, g, sem):
        d = owner(x, g)
        pltpu.make_async_copy(tiles.at[d], tv.at[d], sem).start()

    def pair(j):
        return [2 * (j % (nx // 2)) + i for i in range(2)]

    def turn(j):
        return pair(j), ((j // (nx // 2)) + 2) % 4 + 1

    for g in range(3):
        tile_load(mx, g, tsem.at[0])

    @pl.loop(0, nx // 2)
    def _(j):
        for k in pair(j):
            tile_load(xat(k + 1), 7, tsem.at[1 + j])

    @pl.loop(0, 2 * nx)
    def _(j):
        ks, t = turn(j)
        for k in ks:
            tile_load(xat(k + 1), t + 2, tsem.at[1 + nx // 2 + j])

    @pl.loop(0, nx - 1)
    def _(k):
        for g in range(3):
            tile_load(xat(k + 1), g, tsem.at[1 + nx // 2 + 2 * nx + k])

    for copy in loads[3:]:
        copy.start()
    for copy in loads[:3]:
        copy.wait()
    for b in range(nblk):
        hi, lo = split(feats[:, b * TB:(b + 1) * TB])
        fs[b, :F, :TB] = hi
        fs[b, :F, TB:] = hi
        fs[b, F:, :TB] = lo
        fs[b, F:, TB:] = jnp.zeros_like(lo)
    acc[...] = jnp.zeros_like(acc)
    acc2[...] = jnp.zeros_like(acc2)

    def tile_forward(x, g):
        d = owner(x, g)
        for c in range(CAP):
            halves = jnp.concatenate(split(tv[d, c]), axis=1)
            tb[d, c] = halves
            o = dot(fs[scol[c, d]], halves, NT_DIMS)
            res = o[:F] + o[F:]
            for h in range(NCH):
                sb[h, x, 4 * g + c] = res[h * FC:(h + 1) * FC]

    drain(tv.at[pl.ds(0, 3)], tsem.at[0])
    for g in range(3):
        tile_forward(mx, g)
    pl.semaphore_wait(barrier, 7 * nx - 1 + 1 + nf - 1)

    def m_copy(i):
        return remote(rrow, rtab.at[i], mss, mrs, node=mx * nz + zat(2 * i - 1))

    for i in range(2):
        m_copy(i).start()

    def x_copy(to):
        cols = pl.ds(pl.multiple_of(to * (Q * TB), Q * TB), Q * TB)
        rows = pl.ds(pl.multiple_of(mf * F, F), F)
        return remote(feats.at[:, cols], xall.at[rows, :], xss, xrs, feat=to)

    @pl.loop(1, nf)
    def _(k):
        x_copy((mf + k) % nf).start()

    own_rows = pl.ds(pl.multiple_of(mf * F, F), F)
    xall[own_rows, :] = feats[:, pl.ds(pl.multiple_of(mf * (Q * TB), Q * TB), Q * TB)]

    def place(t):
        if not isinstance(t, int):
            return pl.ds(4 * t + 8, 4)
        return pl.ds(0, 12) if t == 0 else pl.ds(4 * t + 8, 4) if t < 5 else pl.ds(18 + 2 * t, 2)

    def arrival(per_pair, single, h, k, t):
        return single.at[h, k] if isinstance(t, int) and t == 0 else per_pair.at[h, k // 2, t - 1]

    def f_copy(h, k, t):
        x, at = xat(k + 1), place(t)
        return remote(sb.at[h, x, at], rb.at[h, mx, at], fss.at[k // (nx - 1)], arrival(frs, frn, h, k, t),
                      node=x * nz + zat(shift(t)))

    def b_copy(h, k, t):
        x, at = xat(k + 1), place(t)
        return remote(bsd.at[h, x, at], brv.at[h, mx, at], bss.at[k // (nx - 1)], arrival(brs, brn, h, k, t),
                      node=x * nz + zat(-shift(t)))

    def f_arrived(h, k, t):
        count = 1 if isinstance(t, int) and t == 0 else 2
        drain(rb.at[h, pl.ds(0, count), place(t)], arrival(frs, frn, h, k, t))

    def b_arrived(h, k, t):
        count = 1 if isinstance(t, int) and t == 0 else 2
        drain(brv.at[h, pl.ds(0, count), place(t)], arrival(brs, brn, h, k, t))

    @pl.loop(0, nx // 2)
    def _(j):
        drain(tv.at[pl.ds(0, 2)], tsem.at[1 + j])
        for k in pair(j):
            tile_forward(xat(k + 1), 7)
            f_copy(0, k, 5).start()
            f_copy(0, k, 6).start()

    @pl.loop(0, 2 * nx)
    def _(j):
        ks, t = turn(j)
        drain(tv.at[pl.ds(0, 2)], tsem.at[1 + nx // 2 + j])
        for k in ks:
            tile_forward(xat(k + 1), t + 2)
            f_copy(0, k, t).start()

    @pl.loop(0, nx - 1)
    def _(k):
        drain(tv.at[pl.ds(0, 3)], tsem.at[1 + nx // 2 + 2 * nx + k])
        for g in range(3):
            tile_forward(xat(k + 1), g)
        f_copy(0, k, 0).start()

    for h in range(1, NCH):
        @pl.loop(0, nx)
        def _(k):
            f_copy(h, k, 5).start()
            f_copy(h, k, 6).start()

        @pl.loop(0, 2 * nx)
        def _(j):
            ks, t = turn(j)
            for k in ks:
                f_copy(h, k, t).start()

        @pl.loop(0, nx - 1)
        def _(k):
            f_copy(h, k, 0).start()

    for copy in loads[3:]:
        copy.wait()
    ws = wself[...]
    wsh[...], wsl[...] = split(ws)
    wsth[...], wstl[...] = split(ws.T)
    for h in range(NCH):
        rows = jnp.concatenate(
            [wneigh[f * F + h * FC:f * F + (h + 1) * FC, :] for f in range(nf)], axis=0)
        wnh[h], wnl[h] = split(rows)
        wnth[h], wntl[h] = split(rows.T)
    for q in range(Q):
        cott[:, q * TB:(q + 1) * TB] = cot[q * TB:(q + 1) * TB, :].T
    bias_t = jnp.broadcast_to(bias[...], (TB, H)).T

    if nf > 1:
        drain(xall.at[pl.ds(0, (nf - 1) * F)], xrs)
    for q in range(Q):
        cols = slice(q * TB, (q + 1) * TB)
        pret[:, cols] = bias_t + dot3((wsth[...], wstl[...]), split(xall[:, cols]), NN_DIMS)
    drain(rtab, mrs)

    def add(to, vals, dest):
        tiles_of = [v.reshape(-1, 8, TB) for v in vals]
        wanted = [jnp.full((8, TB), r, jnp.int32) for r in dest]

        @pl.loop(0, nblk // 8)
        def _(k):
            near = [w - k * 8 for w in wanted]
            sums = [to[k * 8 + i].reshape(-1, 8, TB) for i in range(8)]
            for i in range(8):
                parts = [jnp.where((r == i)[None], v, 0.0) for v, r in zip(tiles_of, near)]
                while len(parts) > 1:
                    parts = [a + b for a, b in zip(parts[::2], parts[1::2])] + parts[len(parts) // 2 * 2:]
                sums[i] = sums[i] + parts[0]
            for i in range(8):
                to[k * 8 + i] = sums[i].reshape(to.shape[1:])

    def add_plane(h, x, ref):
        s = x * nz + mz
        for g in range(3):
            rows = [rrow[c, s] if g == 0 else rtab[g - 1, c, s] for c in range(CAP)]
            add(acc.at[g, h], [ref[h, x, 4 * g + c] for c in range(CAP)], rows)

    def d_copy(h, w, i):
        return remote(acc.at[1 + i, h, :, w], dr.at[h, i, :, w], dss, drs.at[h, w], node=mx * nz + zat(1 - 2 * i))

    for h in range(NCH):
        add_plane(h, mx, sb)

        @pl.loop(0, nx // 2)
        def _(j):
            for i in range(2):
                vals, dest = [], []
                f_arrived(h, 2 * j, 5 + i)
                for k in pair(j):
                    x = xat(-1 - k)
                    s = x * nz + zat(-shift(5 + i))
                    vals += [rb[h, x, 28 + 2 * i + c] for c in range(2)]
                    dest += [rtab[i, 2 * i + c, s] for c in range(2)]
                add(acc.at[1 + i, h], vals, dest)

        @pl.loop(0, 2 * nx)
        def _(j):
            ks, t = turn(j)
            side = 1 - t % 2
            vals, dest = [], []
            f_arrived(h, ks[0], t)
            for k in ks:
                x = xat(-1 - k)
                s = x * nz + zat(-shift(t))
                vals += [rb[h, x, 4 * t + 8 + c] for c in range(CAP)]
                dest += [rtab[side, c, s] for c in range(CAP)]
            add(acc.at[1 + side, h], vals, dest)

        @pl.loop(0, nx - 1)
        def _(k):
            f_arrived(h, k, 0)
            add_plane(h, xat(-1 - k), rb)

        for w in range(W):
            for i in range(2):
                d_copy(h, w, i).start()

    def n_copy(h, w, to):
        rows = pl.ds(8 * w, 8)
        return remote(nsd.at[h, to, rows], nall.at[h, mf, rows], nss, nrs.at[h, w], feat=to)

    for h in range(NCH):
        for w in range(W):
            drain(dr.at[h, :, :, w], drs.at[h, w])

            @pl.loop(0, nf)
            def _(f):
                for q in range(Q):
                    b = f * Q + q
                    nsd[h, f, w * 8:(w + 1) * 8, q * TB:(q + 1) * TB] = acc[0, h, b, w] + dr[h, 0, b, w] + dr[h, 1, b, w]

            @pl.loop(1, nf)
            def _(k):
                n_copy(h, w, (mf + k) % nf).start()

        nall[h, mf] = nsd[h, mf]

    inv = [1.0 / deg[mf * Q + q].astype(F32) for q in range(Q)]
    for h in range(NCH):
        for w in range(W if nf > 1 else 0):
            drain(nall.at[h, pl.ds(0, nf - 1), pl.ds(8 * w, 8)], nrs.at[h, w])

        for q in range(Q):
            cols = slice(q * TB, (q + 1) * TB)
            nb = nall[h, :, :, cols].reshape(nf * FC, TB) * inv[q]
            nall[h, :, :, cols] = nb.reshape(nf, FC, TB)
            pre = pret[:, cols] + dot3((wnth[h], wntl[h]), split(nb), NN_DIMS)
            if h < NCH - 1:
                pret[:, cols] = pre
            else:
                sig = 1.0 / (1.0 + jnp.exp(-pre))
                pret[:, cols] = pre * sig
                g = cott[:, cols] * (sig * (1.0 + pre * (1.0 - sig)))
                gh[:, cols], gl[:, cols] = split(g)
    def g_copy(h, w, to):
        blocks, rows = pl.ds(pl.multiple_of(mf * Q, Q), Q), pl.ds(8 * w, 8)
        return remote(gsd.at[h, to, :, rows], grc[h].at[blocks, rows], gss, grs.at[h, w], feat=to)

    for h in range(NCH):
        for q in range(Q):
            cols = slice(q * TB, (q + 1) * TB)
            back = dot3((wnh[h], wnl[h]), (gh[:, cols], gl[:, cols]), NN_DIMS) * inv[q]
            for f in range(nf):
                gsd[h, f, q] = back[f * FC:(f + 1) * FC]

        for w in range(W):
            @pl.loop(1, nf)
            def _(k):
                g_copy(h, w, (mf + k) % nf).start()

        for q in range(Q):
            grc[h][mf * Q + q] = gsd[h, mf, q]

    def r1_copy(to):
        return remote(r1s.at[to], r1r.at[mf], r1ss, r1rs, feat=to)

    part_self = dot3(split(xall[...]), (gh[...], gl[...]), NT_DIMS)
    for f in range(nf):
        r1s[f, :F] = part_self[f * F:(f + 1) * F]
    for h in range(NCH):
        part = dot3(split(nall[h].reshape(nf * FC, Q * TB)), (gh[...], gl[...]), NT_DIMS)
        for f in range(nf):
            r1s[f, F + h * FC:F + (h + 1) * FC] = part[f * FC:(f + 1) * FC]
    ones = jnp.ones((16, Q * TB), BF)
    part_bias = (dot(ones, gh[...], NT_DIMS) + dot(ones, gl[...], NT_DIMS))[:8]
    for f in range(nf):
        r1s[f, 2 * F:] = part_bias

    @pl.loop(1, nf)
    def _(k):
        r1_copy((mf + k) % nf).start()

    r1r[mf] = r1s[mf]

    def e_copy(h, w, i):
        rows = pl.ds(8 * w, 8)
        return remote(grc[h].at[:, rows], gnb[h][i].at[:, rows], ess, ers.at[h], node=mx * nz + zat(2 * i - 1))

    for h in range(NCH):
        for w in range(W):
            if nf > 1:
                drain(grc[h].at[pl.ds(0, (nf - 1) * Q), pl.ds(8 * w, 8)], grs.at[h, w])
            for i in range(2):
                e_copy(h, w, i).start()

    for q in range(Q):
        cols = slice(q * TB, (q + 1) * TB)
        act_v[cols, :] = pret[:, cols].T
    act_copy = pltpu.make_async_copy(act_v, act_o, osem.at[0])
    act_copy.start()

    def s_copy(to):
        blocks = pl.ds(pl.multiple_of(mf * Q, Q), Q)
        return remote(ssd.at[to], srv.at[blocks], sss, srs, feat=to)

    for q in range(Q):
        cols = slice(q * TB, (q + 1) * TB)
        back = dot3((wsh[...], wsl[...]), (gh[:, cols], gl[:, cols]), NN_DIMS)
        for f in range(nf):
            ssd[f, q] = back[f * F:(f + 1) * F]

    for q in range(Q):
        srv[mf * Q + q] = ssd[mf, q]

    def pick(src, r):
        return src[jnp.maximum(r, 0)] * jnp.where(r >= 0, 1.0, 0.0)

    def pick_plane(h, x, ref):
        s = x * nz + mz
        for g in range(3):
            src = grc[h] if g == 0 else gnb[h][g - 1]
            for c in range(CAP):
                ref[h, x, 4 * g + c] = pick(src, rrow[c, s] if g == 0 else rtab[g - 1, c, s])

    def pick_far(h):
        drain(acc.at[pl.ds(0, 2), h], ers.at[h])

        @pl.loop(0, nx)
        def _(j):
            x = xat(j + 1)
            for i in range(2):
                s = x * nz + zat(-shift(5 + i))
                for c in range(2):
                    bsd[h, x, 28 + 2 * i + c] = pick(gnb[h][i], rtab[i, 2 * i + c, s])
                b_copy(h, j, 5 + i).start()

        for t in (3, 4, 1, 2):
            @pl.loop(0, nx)
            def _(j):
                x = xat(j + 1)
                s = x * nz + zat(-shift(t))
                side = 1 - t % 2
                for c in range(CAP):
                    bsd[h, x, 4 * t + 8 + c] = pick(gnb[h][side], rtab[side, c, s])
                b_copy(h, j, t).start()

    def pick_near(h):
        @pl.loop(0, nx - 1)
        def _(j):
            x = xat(j + 1)
            pick_plane(h, x, bsd)
            b_copy(h, j, 0).start()

        pick_plane(h, mx, brv)

    HALF = NCH // 2

    if nf > 1:
        drain(r1r.at[pl.ds(0, nf - 1)], r1rs)
    bias_sum = sum((r1r[f, 2 * F:] for f in range(1, nf)), r1r[0, 2 * F:])
    for z in range(nz):
        rows = slice(z * RZ, (z + 1) * RZ)
        r2s[z, :RZ] = sum((r1r[f, rows] for f in range(1, nf)), r1r[0, rows])
        r2s[z, RZ:] = bias_sum

    def r2_copy(z):
        return remote(r2s.at[z], r2r.at[mz], r2ss, r2rs, node=mx * nz + z)

    @pl.loop(1, nz)
    def _(k):
        r2_copy(zat(k)).start()

    r2r[mz] = r2s[mz]
    for h in range(HALF):
        pick_far(h)
    @pl.loop(1, nf)
    def _(k):
        s_copy((mf + k) % nf).start()

    drain(r2r.at[pl.ds(0, nz - 1)], r2rs)
    r3s[...] = total(r2r, nz)

    def r3_copy(x):
        return remote(r3s, r3r.at[mx], r3ss, r3rs, node=x * nz + mz)

    @pl.loop(1, nx)
    def _(k):
        r3_copy(xat(k)).start()

    r3r[mx] = r3s[...]
    for h in range(HALF):
        pick_near(h)

    others = (nf - 1) * nz // 2
    if nf > 1:
        drain(xall.at[pl.ds(0, (nf - 1) * F)], xss)
        drain(r1s.at[pl.ds(0, nf - 1)], r1ss)
        drain(nsd.at[:, pl.ds(0, nf - 1)], nss)
        drain(gsd.at[:, pl.ds(0, nf - 1)], gss)
    drain(sb.at[:, pl.ds(0, nx - 1)], fss.at[0])
    drain(sb.at[:, 0, pl.ds(0, 20)], fss.at[1])
    drain(acc.at[pl.ds(0, 2)], dss)
    drain(acc.at[pl.ds(0, 2)], ess)
    drain(rtab, mss)
    drain(r2r.at[pl.ds(0, nz - 1)], r2ss)

    def tile_backward(p, groups):
        outs, dest = [], []
        for x, g in groups:
            d = owner(x, g)
            for c in range(CAP):
                a = jnp.concatenate([brv[h, x, 4 * g + c] for h in range(p * HALF, (p + 1) * HALF)], axis=0)
                o = dot(jnp.concatenate(split(a), axis=0), tb[d, c], NN_DIMS)
                outs.append(o[:F // 2, :TB] + o[F // 2:, :TB] + o[:F // 2, TB:])
                dest.append(scol[c, d])
        add(acc2.at[p], outs, dest)

    def arrived(p, k, t):
        for h in range(p * HALF, (p + 1) * HALF):
            b_arrived(h, k, t)

    def near(p):
        @pl.loop(0, nx - 1)
        def _(k):
            arrived(p, k, 0)
            tile_backward(p, [(xat(-1 - k), g) for g in range(3)])

    def far(p):
        @pl.loop(0, nx // 2)
        def _(j):
            arrived(p, 2 * j, 5)
            arrived(p, 2 * j, 6)
            tile_backward(p, [(xat(-1 - k), 7) for k in pair(j)])

    def middle(p, start, stop):
        @pl.loop(start, stop)
        def _(j):
            ks, t = turn(j)
            arrived(p, ks[0], t)
            tile_backward(p, [(xat(-1 - k), t + 2) for k in ks])

    tile_backward(0, [(mx, g) for g in range(3)])
    drain(r3r.at[pl.ds(0, nx - 1)], r3rs)
    grads = total(r3r, nx)
    r4s[...] = grads[:RZ]
    gb_v[...] = grads[RZ:RZ + 1]

    def r4_copy(z):
        return remote(r4s, r4r.at[mz], r4ss, r4rs, node=mx * nz + z)

    @pl.loop(1, nz)
    def _(k):
        r4_copy(zat(k)).start()

    r4r[mz] = r4s[...]
    for h in range(HALF, NCH):
        pick_far(h)
        pick_near(h)
    tile_backward(1, [(mx, g) for g in range(3)])
    far(0)
    middle(0, 0, 2 * nx)
    near(0)

    drain(r4r.at[pl.ds(0, nz - 1)], r4rs)
    drain(r3r.at[pl.ds(0, nx - 1)], r3ss)
    if nf > 1:
        drain(ssd.at[pl.ds(0, nf - 1)], sss)

    def r5_copy(i, to):
        part = r4r.at[pl.ds(i * (nz // 2), nz // 2)]
        rows = pl.ds(pl.multiple_of(mf * (nz // 2), nz // 2), nz // 2)
        return remote(part, outw.at[i, rows], r5ss, r5rs, feat=to)

    for i in range(2):
        @pl.loop(1, nf)
        def _(k):
            r5_copy(i, (mf + k) % nf).start()

        for z in range(nz // 2):
            outw[i, mf * (nz // 2) + z] = r4r[i * (nz // 2) + z]
    near(1)
    far(1)
    middle(1, 0, 2 * nx)

    if nf > 1:
        drain(srv.at[pl.ds(0, (nf - 1) * Q)], srs)
    for b in range(nblk):
        gf_v[:, b * TB:(b + 1) * TB] = srv[b] + jnp.concatenate([acc2[0, b], acc2[1, b]], axis=0)
    gf_copy = pltpu.make_async_copy(gf_v, gf_o, osem.at[1])
    gf_copy.start()
    if nf > 1:
        drain(outw.at[:, pl.ds(0, others)], r5rs)
    tail = [
        pltpu.make_async_copy(outw.at[0], gs_o, osem.at[2]),
        pltpu.make_async_copy(outw.at[1], gn_o, osem.at[3]),
        pltpu.make_async_copy(gb_v, gb_o, osem.at[4]),
    ]
    for copy in tail:
        copy.start()

    if nf > 1:
        drain(outw.at[:, pl.ds(0, others)], r5ss)
    drain(r4r.at[pl.ds(0, nz - 1)], r4ss)
    drain(bsd.at[:, pl.ds(0, nx - 1)], bss.at[0])
    drain(bsd.at[:, 0, pl.ds(0, 20)], bss.at[1])
    act_copy.wait()
    gf_copy.wait()
    for copy in tail:
        copy.wait()


def hand_over(*refs):
    n = (len(refs) - 1) // 3
    sem = refs[-1]
    takes = [pltpu.make_async_copy(refs[i], refs[2 * n + i], sem.at[0, i]) for i in range(n)]
    gives = [pltpu.make_async_copy(refs[2 * n + i], refs[n + i], sem.at[1, i]) for i in range(n)]
    for take in takes:
        take.start()
    for take, give in zip(takes, gives):
        take.wait()
        give.start()
    for give in gives:
        give.wait()


def shards(nn, nf, nx, node_feats, tiles, send_col, recv_row, degree, w_self, w_neigh, bias, cotangent):
    F, owned = node_feats.shape
    nz = nn // nx
    nblk = owned // TB
    Q = nblk // nf
    H = w_self.shape[0]
    FC = F // NCH
    RZ = 2 * F // nz
    cols = Q * TB
    slots = nz * CAP
    anyw = pl.BlockSpec(memory_space=pl.ANY)
    V, D = pltpu.VMEM, pltpu.SemaphoreType.DMA
    scratch = [
        V((F, owned), F32), pltpu.SMEM((CAP, nn), jnp.int32), pltpu.SMEM((CAP, nn), jnp.int32),
        V((nblk, 1, TB), jnp.int32), V((H, H), F32), V((H, H), F32),
        V((1, H), F32), V((cols, H), F32),
        V((nn, CAP, TB, TB), F32), V((nn, CAP, TB, 2 * TB), BF),
        V((nblk, 2 * F, 2 * TB), BF),
        V((NCH, nx, slots, FC, TB), F32), V((NCH, nx, slots, FC, TB), F32),
        V((3, NCH, nblk, FC // 8, 8, TB), F32), V((NCH, 2, nblk, FC // 8, 8, TB), F32),
        V((H, cols), F32),
        V((NCH, nf, FC, cols), F32), V((NCH, nf, FC, cols), F32),
        V((H, H), BF), V((H, H), BF), V((H, H), BF), V((H, H), BF),
        V((NCH, H // NCH, H), BF), V((NCH, H // NCH, H), BF),
        V((NCH, H, H // NCH), BF), V((NCH, H, H // NCH), BF),
        V((H, cols), F32), V((H, cols), F32),
        V((H, cols), BF), V((H, cols), BF),
        V((cols, H), F32),
        V((NCH, nf, Q, FC, TB), F32),
        [V((nblk, FC, TB), F32) for _ in range(NCH)],
        [[V((nblk, FC, TB), F32) for _ in range(2)] for _ in range(NCH)],
        V((nf, Q, F, TB), F32), V((nblk, F, TB), F32),
        V((NCH, nx, slots, FC, TB), F32), V((NCH, nx, slots, FC, TB), F32),
        V((2, nblk, F // 2, TB), F32), V((F, owned), F32),
        V((nf, 2 * F + 8, H), F32), V((nf, 2 * F + 8, H), F32),
        V((nz, RZ + 8, H), F32), V((nz, RZ + 8, H), F32),
        V((RZ + 8, H), F32), V((nx, RZ + 8, H), F32),
        V((RZ, H), F32), V((nz, RZ, H), F32),
        V((2, nf * nz // 2, RZ, H), F32), V((1, H), F32),
        pltpu.SMEM((2, CAP, nn), jnp.int32),
        D((8,)), D((3 * nx + nx // 2,)),
        D, D, D, D,
        D((2,)), D((NCH, nx // 2, 6)), D((NCH, nx - 1)),
        D, D((NCH, FC // 8)), D, D((NCH, FC // 8)), D, D((NCH, FC // 8)),
        D, D((NCH,)), D, D,
        D((2,)), D((NCH, nx // 2, 6)), D((NCH, nx - 1)),
        *[D] * 10,
        D((5,)),
    ]
    act, gf, gs, gn, gb = pl.pallas_call(
        functools.partial(kernel, nn, nf, nx),
        out_shape=[
            jax.ShapeDtypeStruct((cols, H), F32),
            jax.ShapeDtypeStruct((F, owned), F32),
            jax.ShapeDtypeStruct((nf * nz // 2, RZ, H), F32),
            jax.ShapeDtypeStruct((nf * nz // 2, RZ, H), F32),
            jax.ShapeDtypeStruct((1, H), F32),
        ],
        in_specs=[anyw] * 9,
        out_specs=[anyw] * 5,
        scratch_shapes=scratch,
        compiler_params=pltpu.CompilerParams(
            collective_id=0, has_side_effects=True, vmem_limit_bytes=62 * 1024 * 1024
        ),
    )(
        node_feats, tiles, send_col.T, recv_row.T, degree.reshape(nblk, 1, TB),
        w_self, w_neigh, bias.reshape(1, H), cotangent,
    )
    results = [act, gf, gs.reshape(H, H), gn.reshape(H, H), gb]
    act, gf, gs, gn, gb = pl.pallas_call(
        hand_over,
        out_shape=[jax.ShapeDtypeStruct(r.shape, r.dtype) for r in results],
        in_specs=[anyw] * 5,
        out_specs=[anyw] * 5,
        scratch_shapes=[V(r.shape, r.dtype) for r in results] + [D((2, 5))],
        compiler_params=pltpu.CompilerParams(vmem_limit_bytes=62 * 1024 * 1024),
    )(*results)
    return act, gf, gs, gn, gb.reshape(H)


def solution(mesh):
    return jax.shard_map(
        functools.partial(shards, mesh.shape["node"], mesh.shape["feat"], NX),
        mesh=mesh,
        in_specs=(
            P("feat", "node"),
            P("node", None, None, None),
            P("node", None),
            P("node", None),
            P("node"),
            P(),
            P(),
            P(),
            P(("node", "feat"), None),
        ),
        out_specs=(P(("node", "feat"), None), P("feat", "node"), P(), P(), P()),
        check_vma=False,
    )
```
